32 devices in a mesh: layers: 2 (over y), blk: 4 (over z), tok: 4 (over x, core).
Axes of the slice: x: 2, y: 2, z: 4, core: 2. Of those that a mesh axis runs over, the one named last changes fastest.
Arguments:
- inputs: bfloat16 [8192, 1024], P(('layers', 'blk', 'tok')), parts along dimension 0, may hold values from -6 to 6
- targets: bfloat16 [8192, 1024], P(('layers', 'blk', 'tok')), parts along dimension 0, may hold values from -6 to 6
- mask: int32 [8192, 128], P(('layers', 'blk', 'tok')), parts along dimension 0, may hold values from 0 to 1, as said below
- enc_weight: bfloat16 [256, 1024], P(('layers', 'blk')), parts along dimension 0, may hold values from -0.1875 to 0.1875
- enc_bias: bfloat16 [256], P(('layers', 'blk')), parts along dimension 0, may hold values from -3 to 3
- dec_weight: bfloat16 [256, 1024], P(('layers', 'blk')), parts along dimension 0, may hold values from -0.5 to 0.5
- dec_bias: float32 [2048], P('layers'), parts along dimension 0, may hold values from -3 to 3
Outputs:
- recon: bfloat16 [8192, 1024], P(('layers', 'blk', 'tok')), parts along dimension 0
- grad_enc: float32 [256, 1024], P(('layers', 'blk'), 'tok'), parts along dimension 0
- grad_dec: float32 [256, 1024], P(('layers', 'blk'), 'tok'), parts along dimension 0
The draws below stay inside these ranges and needn't reach their ends.
There are 2 independent parts, one for each index of `layers`. The reference program is written for one: setup_inputs(seed, part) draws one part's arguments, and reference() takes and returns one part's arrays. A program takes and returns all parts, laid end to end along the dimension named above; each array names one. Nothing has to cross between parts.
Inputs may be any that keep to these rules, and one draw needn't show every extreme that they name: `mask`: each block of 256 tokens (one device's) by 32 latents is either all zero or holds independent 0 and 1 entries; how many blocks are live differs between devices.
All inputs are finite; a program needn't handle non-finite values.
Results may differ from the reference program's by a relative error of at most 0.0095.
Values may be sent and summed in bfloat16 or wider, within the bound.
No kernel may reach another device: no remote copies, remote signals or barrier semaphores. Data moves between devices by JAX's collectives and lax.ppermute only.
A program may use at most 64 MiB of HBM per device.

```python
import math
import jax
import jax.numpy as jnp

D = 1024
TOK_DEV = 256
LAT_DEV = 32
LATENTS = 128
TOKENS = 4096


def draw_mask(key, part):
    key = jax.random.fold_in(key, 7)
    key_level, key_block, key_inner = jax.random.split(key, 3)
    row_blocks = TOKENS // TOK_DEV
    col_blocks = LATENTS // LAT_DEV
    level = jax.random.randint(key_level, (row_blocks, 1), 1, 4)
    blocks = (jax.random.randint(key_block, (row_blocks, col_blocks), 0, 4) < level).astype(jnp.int32)
    spread = jnp.repeat(jnp.repeat(blocks, TOK_DEV, axis=0), LAT_DEV, axis=1)
    inner = jax.random.randint(key_inner, (TOKENS, LATENTS), 0, 2)
    return (spread * inner).astype(jnp.int32)


def levels(key, shape, cuts, least, high):
    def one(axis_at, blocks):
        draws = jax.random.uniform(jax.random.fold_in(jax.random.fold_in(key, 6), axis_at), (blocks,), jnp.float32, least / len(cuts), high / len(cuts))
        return jnp.repeat(jnp.exp(draws), shape[axis_at] // blocks).reshape((-1,) + (1,) * (len(shape) - axis_at - 1))

    level = one(*cuts[0])
    for cut in cuts[1:]:
        level = level * one(*cut)
    return level


def scatter_about(key, shape, deviation, reach, pieces=(), kind=jnp.bfloat16):
    loudness = levels(key, shape, pieces, -0.22, 0.18) if pieces else 1.0
    result = jax.random.normal(key, shape, jnp.float32) * deviation * loudness
    return jnp.minimum(jnp.maximum(result, -reach), reach).astype(kind)


def setup_inputs(seed: int = 0, part: int = 0) -> dict:
    keys = jax.random.split(jax.random.key(seed), 8)
    part_keys = jax.random.split(jax.random.fold_in(keys[7], part), 8)
    inputs = scatter_about(part_keys[0], (TOKENS, D), 1.0, 6.0, ((0, 16),))
    targets = scatter_about(part_keys[1], (TOKENS, D), 1.0, 6.0, ((0, 16),))
    mask = draw_mask(jax.random.fold_in(jax.random.fold_in(keys[7], part), 71), part)
    enc_weight = scatter_about(part_keys[3], (LATENTS, D), D ** -0.5, 0.1875, ((0, 4),))
    enc_bias = scatter_about(part_keys[4], (LATENTS,), 0.5, 3.0, ((0, 4),))
    dec_weight = scatter_about(part_keys[5], (LATENTS, D), LATENTS ** -0.5, 0.5, ((0, 4),))
    dec_bias = scatter_about(part_keys[6], (D,), 0.5, 3.0, (), jnp.float32)
    return dict(inputs=inputs, targets=targets, mask=mask, enc_weight=enc_weight, enc_bias=enc_bias, dec_weight=dec_weight, dec_bias=dec_bias)


def reference(inputs, targets, mask, enc_weight, enc_bias, dec_weight, dec_bias):
    gate = mask.astype(jnp.float32)
    pre = jnp.dot(inputs, enc_weight.T, preferred_element_type=jnp.float32) + enc_bias.astype(jnp.float32)[None, :]
    act = (pre * gate).astype(jnp.bfloat16)
    recon_full = jnp.dot(act, dec_weight, preferred_element_type=jnp.float32) + dec_bias[None, :]
    error = (recon_full - targets.astype(jnp.float32)).astype(jnp.bfloat16)
    back = jnp.dot(error, dec_weight.T, preferred_element_type=jnp.float32)
    dpre = (back * gate).astype(jnp.bfloat16)
    factor = 1.0 / math.sqrt(TOKENS)
    grad_enc = jnp.dot(dpre.T, inputs, preferred_element_type=jnp.float32) * factor
    grad_dec = jnp.dot(act.T, error, preferred_element_type=jnp.float32) * factor
    return (recon_full.astype(jnp.bfloat16), grad_enc, grad_dec)
```

```python
import math

import jax
import jax.numpy as jnp
from jax import lax
from jax.experimental import pallas as pl
from jax.experimental.pallas import tpu as pltpu
from jax.sharding import PartitionSpec as P

BF16 = jnp.bfloat16
F32 = jnp.float32
VMEM = pl.BlockSpec(memory_space=pltpu.VMEM)
PAIR = ("blk", "tok")

CORE_0 = ((3, 1), (3, 0), (1, 1), (0, 1))
CORE_1 = ((2, 1), (2, 0), (1, 0), (0, 0))


def in_vmem(array):
    return pltpu.with_memory_space_constraint(array, pltpu.VMEM)


def kernel_call(kernel, outs, *operands, scratch=(), flops=0):
    return pl.pallas_call(
        kernel,
        out_shape=outs,
        in_specs=[VMEM] * len(operands),
        out_specs=[VMEM] * len(outs),
        scratch_shapes=list(scratch),
        cost_estimate=pl.CostEstimate(flops=flops, bytes_accessed=0, transcendentals=0),
        compiler_params=pltpu.CompilerParams(vmem_limit_bytes=32 * 1024 * 1024),
    )(*[in_vmem(operand) for operand in operands])


def move(array, blks, toks, where):
    pairs = []
    for b in range(blks):
        for t in range(toks):
            to = where(b, t)
            if to is not None:
                pairs.append((b * toks + t, to[0] * toks + to[1]))
    return lax.ppermute(array, PAIR, pairs)


def pick(core, a, b):
    return jnp.where(core == 0, a, b)


def pack_kernel(enc, dec, bias, whole, half, sems):
    rows, width = enc.shape
    core = lax.axis_index("tok") % 2
    copies = [
        pltpu.make_async_copy(enc, whole.at[pl.ds(0, rows), pl.ds(0, width)], sems.at[0]),
        pltpu.make_async_copy(dec, whole.at[pl.ds(rows, rows), pl.ds(0, width)], sems.at[1]),
    ]
    for copy in copies:
        copy.start()
    side = jnp.broadcast_to(bias[...].reshape(1, rows), (2 * rows, rows)).astype(F32)
    side = jnp.concatenate([side, jnp.zeros((2 * rows, 128 - rows), F32)], axis=1).astype(BF16)
    whole[:, width:] = side
    half[:, width:] = side[:rows]
    for copy in copies:
        copy.wait()

    @pl.when(core == 0)
    def _():
        half[:, :width] = whole[:rows, :width]

    @pl.when(core == 1)
    def _():
        half[:, :width] = whole[rows:, :width]


def step_kernel(
    inputs, targets, mask, enc, dec, bias, dec_bias, one, one_other, far, far_other,
    recon, send, keep, enc_all, dec_all, bias_all, enc_terms, dec_terms,
):
    rows, width = enc.shape
    latents = mask.shape[1]
    rank = lax.axis_index("blk")
    tok = lax.axis_index("tok")
    core = tok % 2
    chip = tok // 2
    lanes = lax.broadcasted_iota(jnp.int32, (8, latents), 1)

    def at(block):
        return pl.ds(pl.multiple_of(block * rows, rows), rows)

    def put(block, enc_from, dec_from, side):
        enc_all[at(block), :] = enc_from
        dec_all[at(block), :] = dec_from
        mine = (lanes >= block * rows) & (lanes < block * rows + rows)
        moved = pltpu.roll(side.astype(F32), block * rows, axis=1)
        bias_all[...] = jnp.where(mine, moved, bias_all[...])

    bias_all[...] = jnp.zeros_like(bias_all)
    own = jnp.broadcast_to(bias[...].reshape(1, rows), (8, rows)).astype(F32)
    own = jnp.concatenate([own, jnp.zeros((8, latents - rows), F32)], axis=1)
    put(rank, enc[...], dec[...], own)

    def unpack(enc_half, dec_half, first, second):
        put(rank ^ 1, enc_half[:, :width], dec_half[:, :width], enc_half[0:16, width:][:8])
        put(rank ^ 3, first[:rows, :width], first[rows:, :width], first[0:16, width:][:8])
        put(rank ^ 2, second[:rows, :width], second[rows:, :width], second[0:16, width:][:8])

    @pl.when(core == 0)
    def _():
        unpack(one, one_other, far, far_other)

    @pl.when(core == 1)
    def _():
        unpack(one_other, one, far_other, far)

    gate = mask[...].astype(F32)
    pre = lax.dot_general(
        inputs[...], enc_all[...], (((1,), (1,)), ((), ())), preferred_element_type=F32
    )
    act = ((pre + bias_all[0:1, :]) * gate).astype(BF16)
    recon_full = jnp.dot(act, dec_all[...], preferred_element_type=F32)
    recon_full = recon_full + dec_bias[...].reshape(1, width)
    recon[...] = recon_full.astype(BF16)
    error = (recon_full - targets[...].astype(F32)).astype(BF16)
    back = lax.dot_general(
        error, dec_all[...], (((1,), (1,)), ((), ())), preferred_element_type=F32
    )
    dpre = (back * gate).astype(BF16)
    enc_terms[...] = lax.dot_general(
        dpre, inputs[...], (((0,), (0,)), ((), ())), preferred_element_type=F32
    )
    dec_terms[...] = lax.dot_general(
        act, error, (((0,), (0,)), ((), ())), preferred_element_type=F32
    )
    share = send.shape[1]
    for i, (zero, other) in enumerate(zip(CORE_0, CORE_1, strict=True)):
        for out, a, b in ((keep, zero, other), (send, other, zero)):
            block = rank ^ pick(core, a[0], b[0])
            to = chip ^ pick(core, a[1], b[1])
            for quarter in range(2):
                cols = pl.ds(pl.multiple_of((to * 2 + quarter) * share, share), share)
                for k, terms in enumerate((enc_terms, dec_terms)):
                    start = (i * 4 + quarter * 2 + k) * rows
                    out[start : start + rows, :] = terms[at(block), cols].astype(BF16)


def add_kernel(keep, came, *pieces):
    rows = pieces[0].shape[0]
    for i, piece in enumerate(pieces):
        span = slice(i * rows, (i + 1) * rows)
        piece[...] = (keep[span, :].astype(F32) + came[span, :].astype(F32)).astype(BF16)


def owner_kernel(a, b, c, d, own, send, keep):
    rows = keep.shape[0]
    core = lax.axis_index("tok") % 2

    def total(last):
        return (
            a[...].astype(F32) + b[...].astype(F32) + c[...].astype(F32) + last[...].astype(F32)
        )

    @pl.when(core == 0)
    def _():
        whole = total(d)
        keep[...] = whole[:rows]
        send[...] = whole[rows:].astype(BF16)

    @pl.when(core == 1)
    def _():
        whole = total(own)
        keep[...] = whole[rows:]
        send[...] = whole[:rows].astype(BF16)


def last_kernel(factor, keep, came, grad_enc, grad_dec):
    rows = grad_enc.shape[0]
    total = (keep[...] + came[...].astype(F32)) * factor
    grad_enc[...] = total[:rows]
    grad_dec[...] = total[rows:]


def small_body(inputs, targets, mask, enc_weight, enc_bias, dec_weight, dec_bias):
    blks, toks = lax.axis_size("blk"), lax.axis_size("tok")
    rows, width = enc_weight.shape
    tokens, latents = mask.shape
    share = width // toks
    factor = 1.0 / math.sqrt(tokens * blks * toks)

    def swap(array):
        return move(array, blks, toks, lambda b, t: (b, t ^ 1))

    whole, half = pl.pallas_call(
        pack_kernel,
        out_shape=[pltpu.VMEM((2 * rows, width + 128), BF16), pltpu.VMEM((rows, width + 128), BF16)],
        in_specs=[pl.BlockSpec(memory_space=pl.ANY)] * 2 + [VMEM],
        out_specs=[VMEM] * 2,
        scratch_shapes=[pltpu.SemaphoreType.DMA((2,))],
    )(enc_weight, dec_weight, enc_bias)
    far = move(whole, blks, toks, lambda b, t: (b ^ (3, 2)[t % 2], t))
    one = move(half, blks, toks, lambda b, t: (b ^ 1, t))
    one_other = swap(one)
    far_other = swap(far)

    recon, send, keep = kernel_call(
        step_kernel,
        [
            pltpu.VMEM((tokens, width), BF16),
            pltpu.VMEM((16 * rows, share), BF16),
            pltpu.VMEM((16 * rows, share), BF16),
        ],
        inputs, targets, mask, enc_weight, dec_weight, enc_bias, dec_bias, one, one_other, far, far_other,
        scratch=[
            pltpu.VMEM((latents, width), BF16),
            pltpu.VMEM((latents, width), BF16),
            pltpu.VMEM((8, latents), F32),
            pltpu.VMEM((latents, width), F32),
            pltpu.VMEM((latents, width), F32),
        ],
        flops=10 * tokens * latents * width,
    )
    came = swap(send)
    pieces = kernel_call(add_kernel, [pltpu.VMEM((4 * rows, share), BF16)] * 4, keep, came)
    arrived = []
    for i, (zero, other) in enumerate(zip(CORE_0, CORE_1, strict=True)):

        def where(b, t, steps=(zero, other)):
            blk, chip = steps[t % 2]
            return None if (blk, chip) == (0, 0) else (b ^ blk, t ^ (2 * chip))

        arrived.append(move(pieces[i], blks, toks, where))
    send, keep = kernel_call(
        owner_kernel,
        [pltpu.VMEM((2 * rows, share), BF16), pltpu.VMEM((2 * rows, share), F32)],
        *arrived, pieces[3],
    )
    came = swap(send)
    grad_enc, grad_dec = kernel_call(
        lambda *refs: last_kernel(factor, *refs),
        [jax.ShapeDtypeStruct((rows, share), F32)] * 2,
        keep, came,
    )
    return recon, grad_enc, grad_dec


def large_body(inputs, targets, mask, enc_weight, enc_bias, dec_weight, dec_bias):
    gate = mask.astype(F32)
    enc_all = lax.all_gather(enc_weight, "blk", axis=0, tiled=True)
    dec_all = lax.all_gather(dec_weight, "blk", axis=0, tiled=True)
    bias_all = lax.all_gather(enc_bias, "blk", axis=0, tiled=True)
    pre = lax.dot_general(
        inputs, enc_all, (((1,), (1,)), ((), ())), preferred_element_type=F32
    )
    act = ((pre + bias_all.astype(F32)[None, :]) * gate).astype(BF16)
    recon_full = jnp.dot(act, dec_all, preferred_element_type=F32) + dec_bias[None, :]
    error = (recon_full - targets.astype(F32)).astype(BF16)
    back = lax.dot_general(
        error, dec_all, (((1,), (1,)), ((), ())), preferred_element_type=F32
    )
    dpre = (back * gate).astype(BF16)
    total = inputs.shape[0] * lax.axis_size("blk") * lax.axis_size("tok")
    factor = 1.0 / math.sqrt(total)
    grads = []
    for left, right in ((dpre, inputs), (act, error)):
        terms = lax.dot_general(
            left, right, (((0,), (0,)), ((), ())), preferred_element_type=F32
        )
        terms = lax.psum_scatter(terms, "blk", scatter_dimension=0, tiled=True)
        terms = lax.psum_scatter(terms, "tok", scatter_dimension=1, tiled=True)
        grads.append(terms * factor)
    return recon_full.astype(BF16), grads[0], grads[1]


def solution(mesh):
    small = mesh.shape["blk"] == 4 and mesh.shape["tok"] == 4
    tokens = P(("layers", "blk", "tok"), None)
    rows = P(("layers", "blk"), None)
    return jax.shard_map(
        small_body if small else large_body,
        mesh=mesh,
        in_specs=(tokens, tokens, tokens, rows, P(("layers", "blk")), rows, P("layers")),
        out_specs=(tokens, P(("layers", "blk"), "tok"), P(("layers", "blk"), "tok")),
        check_vma=False,
    )
```

```python
import math

import jax
import jax.numpy as jnp
from jax import lax
from jax.experimental import pallas as pl
from jax.experimental.pallas import tpu as pltpu
from jax.sharding import PartitionSpec as P

BF16 = jnp.bfloat16
F32 = jnp.float32
VMEM = pl.BlockSpec(memory_space=pltpu.VMEM)
PAIR = ("blk", "tok")
STRIP = 16
TILE = 128

STEPS = (3, 2, 1, 0)


def in_vmem(array):
    return pltpu.with_memory_space_constraint(array, pltpu.VMEM)


def kernel_call(kernel, outs, *operands, scratch=(), flops=0):
    return pl.pallas_call(
        kernel,
        out_shape=outs,
        in_specs=[VMEM] * len(operands),
        out_specs=[VMEM] * len(outs),
        scratch_shapes=list(scratch),
        cost_estimate=pl.CostEstimate(flops=flops, bytes_accessed=0, transcendentals=0),
        compiler_params=pltpu.CompilerParams(vmem_limit_bytes=32 * 1024 * 1024),
    )(*[in_vmem(operand) for operand in operands])


def move(array, blks, toks, where):
    pairs = []
    for b in range(blks):
        for t in range(toks):
            to = where(b, t)
            if to is not None:
                pairs.append((b * toks + t, to[0] * toks + to[1]))
    return lax.ppermute(array, PAIR, pairs)


def pack_kernel(enc, dec, bias, whole, half, side, sems):
    rows, width = enc.shape
    rank = lax.axis_index("blk")
    core = lax.axis_index("tok") % 2
    strips = rows // STRIP
    copies = [pltpu.make_async_copy(bias, side, sems.at[0])]
    for k, source in enumerate((enc, dec)):
        for i in range(strips):
            j = k * strips + i
            copies.append(
                pltpu.make_async_copy(
                    source.at[pl.ds(i * STRIP, STRIP)], whole.at[:, pl.ds(j * width, width)], sems.at[1 + j]
                )
            )
    for copy in copies:
        copy.start()
    copies[0].wait()
    tile = jnp.broadcast_to(side[...].astype(F32).reshape(1, rows), (STRIP, rows))
    tile = jnp.concatenate([tile, jnp.zeros((STRIP, TILE - rows), F32)], axis=1)
    tile = pltpu.roll(tile, rank * rows, axis=1).astype(BF16)
    whole[:, 2 * strips * width :] = tile
    half[:, strips * width :] = tile
    for copy in copies[1:]:
        copy.wait()

    @pl.when(core == 0)
    def _():
        half[:, : strips * width] = whole[:, : strips * width]

    @pl.when(core == 1)
    def _():
        half[:, : strips * width] = whole[:, strips * width : 2 * strips * width]


def load_kernel(inputs, targets, mask, dec_bias, after, *refs):
    *outs, sems = refs
    parts = (len(outs) - 2) // 2
    copies = []
    for i, source in enumerate((inputs, targets)):
        for j, out in enumerate(outs[i * parts : (i + 1) * parts]):
            rows = out.shape[0]
            copies.append((source.at[pl.ds(j * rows, rows)], out))
    copies += [(mask, outs[-2]), (dec_bias, outs[-1])]
    copies = [pltpu.make_async_copy(*pair, sems.at[i]) for i, pair in enumerate(copies)]
    for copy in copies:
        copy.start()
    for copy in copies:
        copy.wait()


def contract(a, b, over_a, over_b):
    return lax.dot_general(a, b, (((over_a,), (over_b,)), ((), ())), preferred_element_type=F32)


def step_kernel(dec_bias, own, one, one_other, far, far_other, *refs):
    *refs, enc_all, dec_all, error_all, enc_terms, dec_terms = refs
    *refs, own_piece = refs
    refs, pieces = refs[: -len(STEPS)], refs[-len(STEPS) :]
    *refs, recon = refs
    parts = len(refs) // 4
    width = recon.shape[1]
    strips = one.shape[1] // width
    rows = strips * STRIP
    rank = lax.axis_index("blk")
    tok = lax.axis_index("tok")
    core = tok % 2
    chip = tok // 2

    def at(block):
        return pl.ds(pl.multiple_of(block * rows, rows), rows)

    def put(to, block, source, first):
        for i in range(strips):
            span = pl.ds(pl.multiple_of(block * rows + i * STRIP, STRIP), STRIP)
            j = first + i
            to[span, :] = source[:, j * width : (j + 1) * width]

    def unpack(enc_half, dec_half, first, second):
        put(enc_all, rank ^ 1, enc_half, 0)
        put(dec_all, rank ^ 1, dec_half, 0)
        for block, source in ((rank ^ 3, first), (rank ^ 2, second)):
            put(enc_all, block, source, 0)
            put(dec_all, block, source, strips)

    put(enc_all, rank, own, 0)
    put(dec_all, rank, own, strips)

    @pl.when(core == 0)
    def _():
        unpack(one, one_other, far, far_other)

    @pl.when(core == 1)
    def _():
        unpack(one_other, one, far_other, far)

    bias = sum(source[:, -TILE:].astype(F32) for source in (own, one, far, far_other))[0:1, :]
    base = dec_bias[...].reshape(1, width)
    half = pieces[0].shape[1]
    cols = pl.ds(pl.multiple_of((chip ^ core) * half, half), half)
    groups = (refs[: 2 * parts + 1], refs[2 * parts + 1 :])
    tokens = recon.shape[0]
    enc_sum, dec_sum = 0.0, 0.0
    for g, group in enumerate(groups):
        gate_all = group[-1]
        acts, dpres = [], []
        for j in range(parts):
            x, target = group[j], group[parts + j]
            n = x.shape[0]
            span = slice(j * n, (j + 1) * n)
            gate = gate_all[span, :].astype(F32)
            act = ((contract(x[...], enc_all[...], 1, 1) + bias) * gate).astype(BF16)
            recon_full = contract(act, dec_all[...], 1, 0) + base
            if g == 0:
                recon[span, :] = recon_full.astype(BF16)
            error = (recon_full - target[...].astype(F32)).astype(BF16)
            error_all[g * tokens + j * n : g * tokens + (j + 1) * n, :] = error
            dpres.append((contract(error, dec_all[...], 1, 1) * gate).astype(BF16))
            acts.append(act)
        act = jnp.concatenate(acts, axis=0)
        dpre = jnp.concatenate(dpres, axis=0)
        x = jnp.concatenate([part[:, cols] for part in group[:parts]], axis=0)
        dec_sum += contract(act, error_all[g * tokens : (g + 1) * tokens, cols], 0, 0)
        enc_sum += contract(dpre, x, 0, 0)
    enc_terms[...] = enc_sum
    dec_terms[...] = dec_sum
    for step, piece in zip(STEPS, pieces, strict=True):
        piece[:rows, :] = enc_terms[at(rank ^ step), :].astype(BF16)
        piece[rows:, :] = dec_terms[at(rank ^ step), :].astype(BF16)
    own_piece[:rows, :] = enc_terms[at(rank), :]
    own_piece[rows:, :] = dec_terms[at(rank), :]


def owner_kernel(*refs):
    *arrived, own, send, keep = refs
    share = keep.shape[1]
    core = lax.axis_index("tok") % 2
    total = sum(part[...].astype(F32) for part in arrived)

    @pl.when(core == 0)
    def _():
        whole = total + own[...]
        keep[...] = whole[:, :share]
        send[...] = whole[:, share:].astype(BF16)

    @pl.when(core == 1)
    def _():
        keep[...] = total[:, share:]
        send[...] = total[:, :share].astype(BF16)


def last_kernel(factor, keep, came, grad_enc, grad_dec):
    rows = grad_enc.shape[0]
    total = (keep[...] + came[...].astype(F32)) * factor
    grad_enc[...] = total[:rows]
    grad_dec[...] = total[rows:]


def small_body(inputs, targets, mask, enc_weight, enc_bias, dec_weight, dec_bias):
    blks, toks = lax.axis_size("blk"), lax.axis_size("tok")
    rows, width = enc_weight.shape
    tokens, latents = mask.shape
    share = width // toks
    factor = 1.0 / math.sqrt(tokens * blks * toks)

    def swap(array):
        return move(array, blks, toks, lambda b, t: (b, t ^ 1))

    strips = rows // STRIP
    whole, half = pl.pallas_call(
        pack_kernel,
        out_shape=[
            pltpu.VMEM((STRIP, 2 * strips * width + TILE), BF16),
            pltpu.VMEM((STRIP, strips * width + TILE), BF16),
        ],
        in_specs=[pl.BlockSpec(memory_space=pl.ANY)] * 3,
        out_specs=[VMEM] * 2,
        scratch_shapes=[pltpu.VMEM((rows,), BF16), pltpu.SemaphoreType.DMA((1 + 2 * strips,))],
    )(enc_weight, dec_weight, enc_bias)
    far = move(whole, blks, toks, lambda b, t: (b ^ (3, 2)[t % 2], t))
    one = move(half, blks, toks, lambda b, t: (b ^ 1, t))
    parts = 2
    *loaded, dec_bias = pl.pallas_call(
        load_kernel,
        out_shape=[pltpu.VMEM((tokens // parts, width), BF16)] * (2 * parts)
        + [pltpu.VMEM(array.shape, array.dtype) for array in (mask, dec_bias)],
        in_specs=[pl.BlockSpec(memory_space=pl.ANY)] * 4 + [VMEM],
        out_specs=[VMEM] * (2 * parts + 2),
        scratch_shapes=[pltpu.SemaphoreType.DMA((2 * parts + 2,))],
        cost_estimate=pl.CostEstimate(flops=0, bytes_accessed=4 * tokens * width, transcendentals=0),
    )(inputs, targets, mask, dec_bias, in_vmem(one))
    others = [swap(array) for array in loaded]
    one_other = swap(one)
    far_other = swap(far)
    piece = (2 * rows, 2 * share)
    recon, *pieces, own = kernel_call(
        step_kernel,
        [pltpu.VMEM((tokens, width), BF16)]
        + [pltpu.VMEM(piece, BF16)] * len(STEPS)
        + [pltpu.VMEM(piece, F32)],
        dec_bias, whole, one, one_other, far, far_other, *loaded, *others,
        scratch=[
            pltpu.VMEM((latents, width), BF16),
            pltpu.VMEM((latents, width), BF16),
            pltpu.VMEM((2 * tokens, width), BF16),
            pltpu.VMEM((latents, 2 * share), F32),
            pltpu.VMEM((latents, 2 * share), F32),
        ],
        flops=16 * tokens * latents * width,
    )
    arrived = []
    for step, out in zip(STEPS, pieces, strict=True):

        def where(b, t, step=step):
            return None if step == 0 and t % 2 == 0 else (b ^ step, t ^ (2 * (t % 2)))

        arrived.append(move(out, blks, toks, where))
    send, keep = kernel_call(
        owner_kernel,
        [pltpu.VMEM((2 * rows, share), BF16), pltpu.VMEM((2 * rows, share), F32)],
        *arrived, own,
    )
    came = swap(send)
    grad_enc, grad_dec = kernel_call(
        lambda *refs: last_kernel(factor, *refs),
        [jax.ShapeDtypeStruct((rows, share), F32)] * 2,
        keep, came,
    )
    return recon, grad_enc, grad_dec


def large_body(inputs, targets, mask, enc_weight, enc_bias, dec_weight, dec_bias):
    gate = mask.astype(F32)
    enc_all = lax.all_gather(enc_weight, "blk", axis=0, tiled=True)
    dec_all = lax.all_gather(dec_weight, "blk", axis=0, tiled=True)
    bias_all = lax.all_gather(enc_bias, "blk", axis=0, tiled=True)
    pre = lax.dot_general(
        inputs, enc_all, (((1,), (1,)), ((), ())), preferred_element_type=F32
    )
    act = ((pre + bias_all.astype(F32)[None, :]) * gate).astype(BF16)
    recon_full = jnp.dot(act, dec_all, preferred_element_type=F32) + dec_bias[None, :]
    error = (recon_full - targets.astype(F32)).astype(BF16)
    back = lax.dot_general(
        error, dec_all, (((1,), (1,)), ((), ())), preferred_element_type=F32
    )
    dpre = (back * gate).astype(BF16)
    total = inputs.shape[0] * lax.axis_size("blk") * lax.axis_size("tok")
    factor = 1.0 / math.sqrt(total)
    grads = []
    for left, right in ((dpre, inputs), (act, error)):
        terms = lax.dot_general(
            left, right, (((0,), (0,)), ((), ())), preferred_element_type=F32
        )
        terms = lax.psum_scatter(terms, "blk", scatter_dimension=0, tiled=True)
        terms = lax.psum_scatter(terms, "tok", scatter_dimension=1, tiled=True)
        grads.append(terms * factor)
    return recon_full.astype(BF16), grads[0], grads[1]


def solution(mesh):
    small = mesh.shape["blk"] == 4 and mesh.shape["tok"] == 4
    tokens = P(("layers", "blk", "tok"), None)
    rows = P(("layers", "blk"), None)
    return jax.shard_map(
        small_body if small else large_body,
        mesh=mesh,
        in_specs=(tokens, tokens, tokens, rows, P(("layers", "blk")), rows, P("layers")),
        out_specs=(tokens, P(("layers", "blk"), "tok"), P(("layers", "blk"), "tok")),
        check_vma=False,
    )
```

```python
import math

import jax
import jax.numpy as jnp
from jax import lax
from jax.experimental import pallas as pl
from jax.experimental.pallas import tpu as pltpu
from jax.sharding import PartitionSpec as P

BF16 = jnp.bfloat16
F32 = jnp.float32
VMEM = pl.BlockSpec(memory_space=pltpu.VMEM)
PAIR = ("blk", "tok")
STRIP = 16
TILE = 128
CHUNKS = 2

FAR_0, FAR_1, NEAR = ((3, 2, 1, 0), (2, 3, 0, 1), (1, 0, 3, 2))
CORE_0 = ((2, 3, 0, 1), (3, 2, 1, 0), (1, 0, 3, 2), None)
CORE_1 = ((2, 3, 0, 1), (3, 2, 1, 0), (1, 0, 3, 2), (0, 1, 2, 3))


def look_up(table, index):
    value = table[-1]
    for i in range(len(table) - 1):
        value = jnp.where(index == i, table[i], value)
    return value


def sender(table):
    return tuple(table.index(i) for i in range(len(table)))


def in_vmem(array):
    return pltpu.with_memory_space_constraint(array, pltpu.VMEM)


def kernel_call(kernel, outs, *operands, scratch=(), flops=0):
    return pl.pallas_call(
        kernel,
        out_shape=outs,
        in_specs=[VMEM] * len(operands),
        out_specs=[VMEM] * len(outs),
        scratch_shapes=list(scratch),
        cost_estimate=pl.CostEstimate(flops=flops, bytes_accessed=0, transcendentals=0),
        compiler_params=pltpu.CompilerParams(vmem_limit_bytes=32 * 1024 * 1024),
    )(*[in_vmem(operand) for operand in operands])


def move(array, blks, toks, where):
    pairs = []
    for b in range(blks):
        for t in range(toks):
            to = where(b, t)
            if to is not None:
                pairs.append((b * toks + t, to[0] * toks + to[1]))
    return lax.ppermute(array, PAIR, pairs)


def pack_kernel(enc, dec, bias, whole, half, side, sems):
    rows, width = enc.shape
    rank = lax.axis_index("blk")
    core = lax.axis_index("tok") % 2
    strips = rows // STRIP
    copies = [pltpu.make_async_copy(bias, side, sems.at[0])]
    for k, source in enumerate((enc, dec)):
        for i in range(strips):
            j = k * strips + i
            copies.append(
                pltpu.make_async_copy(
                    source.at[pl.ds(i * STRIP, STRIP)], whole.at[:, pl.ds(j * width, width)], sems.at[1 + j]
                )
            )
    for copy in copies:
        copy.start()
    copies[0].wait()
    tile = jnp.broadcast_to(side[...].astype(F32).reshape(1, rows), (STRIP, rows))
    tile = jnp.concatenate([tile, jnp.zeros((STRIP, TILE - rows), F32)], axis=1)
    tile = pltpu.roll(tile, rank * rows, axis=1).astype(BF16)
    whole[:, 2 * strips * width :] = tile
    half[:, strips * width :] = tile
    for copy in copies[1:]:
        copy.wait()

    @pl.when(core == 0)
    def _():
        half[:, : strips * width] = whole[:, : strips * width]

    @pl.when(core == 1)
    def _():
        half[:, : strips * width] = whole[:, strips * width : 2 * strips * width]


def load_kernel(inputs, targets, mask, dec_bias, after, *refs):
    *outs, dec_bias_out, mask_ints, sems = refs
    parts = len(outs) // 2
    width = inputs.shape[1]
    copies = [(mask, mask_ints), (dec_bias, dec_bias_out)]
    for i, source in enumerate((inputs, targets)):
        for j, out in enumerate(outs[i * parts : (i + 1) * parts]):
            rows = out.shape[0]
            copies.append((source.at[pl.ds(j * rows, rows)], out.at[:, pl.ds(0, width)]))
    copies = [pltpu.make_async_copy(*pair, sems.at[i]) for i, pair in enumerate(copies)]
    for copy in copies:
        copy.start()
    copies[0].wait()
    for j, out in enumerate(outs[parts:]):
        rows = out.shape[0]
        out[:, width:] = mask_ints[j * rows : (j + 1) * rows, :].astype(F32).astype(BF16)
    for copy in copies[1:]:
        copy.wait()


def join_kernel(far, one, out):
    out[:, : far.shape[1]] = far[...]
    out[:, far.shape[1] :] = one[...]


def contract(a, b, over_a, over_b):
    return lax.dot_general(a, b, (((over_a,), (over_b,)), ((), ())), preferred_element_type=F32)


def step_kernel(dec_bias, own, one, far, other, *refs):
    *refs, enc_all, dec_all, error_all, enc_terms, dec_terms = refs
    *refs, own_piece = refs
    refs, pieces = refs[: -len(CORE_1)], refs[-len(CORE_1) :]
    *refs, recon = refs
    parts = len(refs) // 4
    tokens, width = recon.shape
    strips = one.shape[1] // width
    rows = strips * STRIP
    far_other = other.at[:, pl.ds(0, far.shape[1])]
    one_other = other.at[:, pl.ds(far.shape[1], one.shape[1])]
    rank = lax.axis_index("blk")
    tok = lax.axis_index("tok")
    core = tok % 2
    chip = tok // 2

    def at(block):
        return pl.ds(pl.multiple_of(block * rows, rows), rows)

    def put(to, block, source, first):
        for i in range(strips):
            span = pl.ds(pl.multiple_of(block * rows + i * STRIP, STRIP), STRIP)
            j = first + i
            to[span, :] = source[:, j * width : (j + 1) * width]

    def unpack(enc_half, dec_half, first, second):
        near = look_up(sender(NEAR), rank)
        put(enc_all, near, enc_half, 0)
        put(dec_all, near, dec_half, 0)
        for table, source in ((FAR_0, first), (FAR_1, second)):
            block = look_up(sender(table), rank)
            put(enc_all, block, source, 0)
            put(dec_all, block, source, strips)

    put(enc_all, rank, own, 0)
    put(dec_all, rank, own, strips)

    @pl.when(core == 0)
    def _():
        unpack(one, one_other, far, far_other)

    @pl.when(core == 1)
    def _():
        unpack(one_other, one, far_other, far)

    bias = sum(source[:, -TILE:].astype(F32) for source in (own, one, far, far_other))[0:1, :]
    base = dec_bias[...].reshape(1, width)
    half = pieces[0].shape[1]
    cols = pl.ds(pl.multiple_of((chip ^ core) * half, half), half)
    groups = (refs[: 2 * parts], refs[2 * parts :])
    enc_sum, dec_sum = 0.0, 0.0
    for g, group in enumerate(groups):
        acts, dpres = [], []
        n = tokens // CHUNKS
        x_all = jnp.concatenate([part[...] for part in group[:parts]], axis=0)
        target_all = jnp.concatenate([part[:, :width] for part in group[parts:]], axis=0)
        gate_all = jnp.concatenate([part[:, width:] for part in group[parts:]], axis=0)
        for j in range(CHUNKS):
            span = slice(j * n, (j + 1) * n)
            x, target = x_all[span], target_all[span]
            gate = gate_all[span].astype(F32)
            act = ((contract(x, enc_all[...], 1, 1) + bias) * gate).astype(BF16)
            recon_full = contract(act, dec_all[...], 1, 0) + base
            if g == 0:
                recon[span, :] = recon_full.astype(BF16)
            error = (recon_full - target.astype(F32)).astype(BF16)
            error_all[g * tokens + j * n : g * tokens + (j + 1) * n, :] = error
            dpres.append((contract(error, dec_all[...], 1, 1) * gate).astype(BF16))
            acts.append(act)
        act = jnp.concatenate(acts, axis=0)
        dpre = jnp.concatenate(dpres, axis=0)
        x = jnp.concatenate([part[:, cols] for part in group[:parts]], axis=0)
        dec_sum += contract(act, error_all[g * tokens : (g + 1) * tokens, cols], 0, 0)
        enc_sum += contract(dpre, x, 0, 0)
    enc_terms[...] = enc_sum
    dec_terms[...] = dec_sum
    for zero, one_table, piece in zip(CORE_0, CORE_1, pieces, strict=True):
        to = look_up(one_table, rank)
        if zero is not None:
            to = jnp.where(core == 0, look_up(zero, rank), to)
        piece[:rows, :] = enc_terms[at(to), :].astype(BF16)
        piece[rows:, :] = dec_terms[at(to), :].astype(BF16)
    own_piece[:rows, :] = enc_terms[at(rank), :]
    own_piece[rows:, :] = dec_terms[at(rank), :]


def owner_kernel(*refs):
    *arrived, own, send, keep = refs
    share = keep.shape[1]
    core = lax.axis_index("tok") % 2
    total = sum(part[...].astype(F32) for part in arrived)

    @pl.when(core == 0)
    def _():
        whole = total + own[...]
        keep[...] = whole[:, :share]
        send[...] = whole[:, share:].astype(BF16)

    @pl.when(core == 1)
    def _():
        keep[...] = total[:, share:]
        send[...] = total[:, :share].astype(BF16)


def last_kernel(factor, keep, came, grad_enc, grad_dec):
    rows = grad_enc.shape[0]
    total = (keep[...] + came[...].astype(F32)) * factor
    grad_enc[...] = total[:rows]
    grad_dec[...] = total[rows:]


def small_body(inputs, targets, mask, enc_weight, enc_bias, dec_weight, dec_bias):
    blks, toks = lax.axis_size("blk"), lax.axis_size("tok")
    rows, width = enc_weight.shape
    tokens, latents = mask.shape
    share = width // toks
    factor = 1.0 / math.sqrt(tokens * blks * toks)

    def swap(array):
        return move(array, blks, toks, lambda b, t: (b, t ^ 1))

    strips = rows // STRIP
    whole, half = pl.pallas_call(
        pack_kernel,
        out_shape=[
            pltpu.VMEM((STRIP, 2 * strips * width + TILE), BF16),
            pltpu.VMEM((STRIP, strips * width + TILE), BF16),
        ],
        in_specs=[pl.BlockSpec(memory_space=pl.ANY)] * 3,
        out_specs=[VMEM] * 2,
        scratch_shapes=[pltpu.VMEM((rows,), BF16), pltpu.SemaphoreType.DMA((1 + 2 * strips,))],
    )(enc_weight, dec_weight, enc_bias)
    far = move(whole, blks, toks, lambda b, t: ((FAR_0, FAR_1)[t % 2][b], t))
    one = move(half, blks, toks, lambda b, t: (NEAR[b], t))
    parts = 2
    *loaded, dec_bias = pl.pallas_call(
        load_kernel,
        out_shape=[pltpu.VMEM((tokens // parts, width), BF16)] * parts
        + [pltpu.VMEM((tokens // parts, width + latents), BF16)] * parts
        + [pltpu.VMEM(dec_bias.shape, F32)],
        in_specs=[pl.BlockSpec(memory_space=pl.ANY)] * 4 + [VMEM],
        out_specs=[VMEM] * (2 * parts + 1),
        scratch_shapes=[pltpu.VMEM(mask.shape, mask.dtype), pltpu.SemaphoreType.DMA((2 * parts + 2,))],
        cost_estimate=pl.CostEstimate(flops=0, bytes_accessed=4 * tokens * width, transcendentals=0),
    )(inputs, targets, mask, dec_bias, in_vmem(half))
    others = [swap(array) for array in loaded]
    joined = kernel_call(
        join_kernel, [pltpu.VMEM((STRIP, 3 * strips * width + 2 * TILE), BF16)], far, one
    )
    other = swap(*joined)
    piece = (2 * rows, 2 * share)
    recon, *pieces, own = kernel_call(
        step_kernel,
        [pltpu.VMEM((tokens, width), BF16)]
        + [pltpu.VMEM(piece, BF16)] * len(CORE_1)
        + [pltpu.VMEM(piece, F32)],
        dec_bias, whole, one, far, other, *loaded, *others,
        scratch=[
            pltpu.VMEM((latents, width), BF16),
            pltpu.VMEM((latents, width), BF16),
            pltpu.VMEM((2 * tokens, width), BF16),
            pltpu.VMEM((latents, 2 * share), F32),
            pltpu.VMEM((latents, 2 * share), F32),
        ],
        flops=16 * tokens * latents * width,
    )
    arrived = []
    for zero, one_table, out in zip(CORE_0, CORE_1, pieces, strict=True):

        def where(b, t, tables=(zero, one_table)):
            table = tables[t % 2]
            return None if table is None else (table[b], t ^ (2 * (t % 2)))

        arrived.append(move(out, blks, toks, where))
    send, keep = kernel_call(
        owner_kernel,
        [pltpu.VMEM((2 * rows, share), BF16), pltpu.VMEM((2 * rows, share), F32)],
        *arrived, own,
    )
    came = swap(send)
    grad_enc, grad_dec = kernel_call(
        lambda *refs: last_kernel(factor, *refs),
        [jax.ShapeDtypeStruct((rows, share), F32)] * 2,
        keep, came,
    )
    return recon, grad_enc, grad_dec


def large_body(inputs, targets, mask, enc_weight, enc_bias, dec_weight, dec_bias):
    gate = mask.astype(F32)
    enc_all = lax.all_gather(enc_weight, "blk", axis=0, tiled=True)
    dec_all = lax.all_gather(dec_weight, "blk", axis=0, tiled=True)
    bias_all = lax.all_gather(enc_bias, "blk", axis=0, tiled=True)
    pre = lax.dot_general(
        inputs, enc_all, (((1,), (1,)), ((), ())), preferred_element_type=F32
    )
    act = ((pre + bias_all.astype(F32)[None, :]) * gate).astype(BF16)
    recon_full = jnp.dot(act, dec_all, preferred_element_type=F32) + dec_bias[None, :]
    error = (recon_full - targets.astype(F32)).astype(BF16)
    back = lax.dot_general(
        error, dec_all, (((1,), (1,)), ((), ())), preferred_element_type=F32
    )
    dpre = (back * gate).astype(BF16)
    total = inputs.shape[0] * lax.axis_size("blk") * lax.axis_size("tok")
    factor = 1.0 / math.sqrt(total)
    grads = []
    for left, right in ((dpre, inputs), (act, error)):
        terms = lax.dot_general(
            left, right, (((0,), (0,)), ((), ())), preferred_element_type=F32
        )
        terms = lax.psum_scatter(terms, "blk", scatter_dimension=0, tiled=True)
        terms = lax.psum_scatter(terms, "tok", scatter_dimension=1, tiled=True)
        grads.append(terms * factor)
    return recon_full.astype(BF16), grads[0], grads[1]


def solution(mesh):
    small = mesh.shape["blk"] == 4 and mesh.shape["tok"] == 4
    tokens = P(("layers", "blk", "tok"), None)
    rows = P(("layers", "blk"), None)
    return jax.shard_map(
        small_body if small else large_body,
        mesh=mesh,
        in_specs=(tokens, tokens, tokens, rows, P(("layers", "blk")), rows, P("layers")),
        out_specs=(tokens, P(("layers", "blk"), "tok"), P(("layers", "blk"), "tok")),
        check_vma=False,
    )
```

```python
import math

import jax
import jax.numpy as jnp
from jax import lax
from jax.experimental import pallas as pl
from jax.experimental.pallas import tpu as pltpu
from jax.sharding import PartitionSpec as P

BF16 = jnp.bfloat16
F32 = jnp.float32
VMEM = pl.BlockSpec(memory_space=pltpu.VMEM)
PAIR = ("blk", "tok")
STRIP = 16
TILE = 128

FAR_0, FAR_1, NEAR = ((3, 2, 1, 0), (2, 3, 0, 1), (1, 0, 3, 2))
CORE_0 = ((2, 3, 0, 1), (3, 2, 1, 0), (1, 0, 3, 2), None)
CORE_1 = ((2, 3, 0, 1), (3, 2, 1, 0), (1, 0, 3, 2), (0, 1, 2, 3))


def look_up(table, index):
    value = table[-1]
    for i in range(len(table) - 1):
        value = jnp.where(index == i, table[i], value)
    return value


def sender(table):
    return tuple(table.index(i) for i in range(len(table)))


def in_vmem(array):
    return pltpu.with_memory_space_constraint(array, pltpu.VMEM)


def kernel_call(kernel, outs, *operands, scratch=(), flops=0):
    return pl.pallas_call(
        kernel,
        out_shape=outs,
        in_specs=[VMEM] * len(operands),
        out_specs=[VMEM] * len(outs),
        scratch_shapes=list(scratch),
        cost_estimate=pl.CostEstimate(flops=flops, bytes_accessed=0, transcendentals=0),
        compiler_params=pltpu.CompilerParams(vmem_limit_bytes=32 * 1024 * 1024),
    )(*[in_vmem(operand) for operand in operands])


def move(array, blks, toks, where):
    pairs = []
    for b in range(blks):
        for t in range(toks):
            to = where(b, t)
            if to is not None:
                pairs.append((b * toks + t, to[0] * toks + to[1]))
    return lax.ppermute(array, PAIR, pairs)


def pack_kernel(enc, dec, bias, whole, half, side, sems):
    rows, width = enc.shape
    rank = lax.axis_index("blk")
    core = lax.axis_index("tok") % 2
    strips = rows // STRIP
    copies = [pltpu.make_async_copy(bias, side, sems.at[0])]
    for k, source in enumerate((enc, dec)):
        for i in range(strips):
            j = k * strips + i
            copies.append(
                pltpu.make_async_copy(
                    source.at[pl.ds(i * STRIP, STRIP)], whole.at[:, pl.ds(j * width, width)], sems.at[1 + j]
                )
            )
    for copy in copies:
        copy.start()
    copies[0].wait()
    tile = jnp.broadcast_to(side[...].astype(F32).reshape(1, rows), (STRIP, rows))
    tile = jnp.concatenate([tile, jnp.zeros((STRIP, TILE - rows), F32)], axis=1)
    tile = pltpu.roll(tile, rank * rows, axis=1).astype(BF16)
    whole[:, 2 * strips * width :] = tile
    half[:, strips * width :] = tile
    for copy in copies[1:]:
        copy.wait()

    @pl.when(core == 0)
    def _():
        half[:, : strips * width] = whole[:, : strips * width]

    @pl.when(core == 1)
    def _():
        half[:, : strips * width] = whole[:, strips * width : 2 * strips * width]


def load_kernel(inputs, targets, mask, dec_bias, after, *refs):
    *outs, dec_bias_out, mask_ints, sems = refs
    parts = len(outs) // 2
    width = inputs.shape[1]
    copies = [(mask, mask_ints), (dec_bias, dec_bias_out)]
    for i, source in enumerate((inputs, targets)):
        for j, out in enumerate(outs[i * parts : (i + 1) * parts]):
            rows = out.shape[0]
            copies.append((source.at[pl.ds(j * rows, rows)], out.at[:, pl.ds(0, width)]))
    copies = [pltpu.make_async_copy(*pair, sems.at[i]) for i, pair in enumerate(copies)]
    for copy in copies:
        copy.start()
    copies[0].wait()
    for j, out in enumerate(outs[parts:]):
        rows = out.shape[0]
        out[:, width:] = mask_ints[j * rows : (j + 1) * rows, :].astype(F32).T.astype(BF16)
    for copy in copies[1:]:
        copy.wait()


def join_kernel(far, one, out):
    out[:, : far.shape[1]] = far[...]
    out[:, far.shape[1] :] = one[...]


def contract(a, b, over_a, over_b):
    return lax.dot_general(a, b, (((over_a,), (over_b,)), ((), ())), preferred_element_type=F32)


def step_kernel(dec_bias, own, one, far, other, *refs):
    *refs, enc_all, dec_all, error_all, act_all, dpre_all, inputs_all, enc_terms, dec_terms = refs
    *refs, own_piece = refs
    refs, pieces = refs[: -len(CORE_1)], refs[-len(CORE_1) :]
    *refs, recon = refs
    parts = len(refs) // 4
    width = recon.shape[1]
    strips = one.shape[1] // width
    rows = strips * STRIP
    far_other = other.at[:, pl.ds(0, far.shape[1])]
    one_other = other.at[:, pl.ds(far.shape[1], one.shape[1])]
    rank = lax.axis_index("blk")
    tok = lax.axis_index("tok")
    core = tok % 2
    chip = tok // 2

    def at(block):
        return pl.ds(pl.multiple_of(block * rows, rows), rows)

    def put(to, block, source, first):
        for i in range(strips):
            span = pl.ds(pl.multiple_of(block * rows + i * STRIP, STRIP), STRIP)
            j = first + i
            to[span, :] = source[:, j * width : (j + 1) * width]

    def unpack(enc_half, dec_half, first, second):
        near = look_up(sender(NEAR), rank)
        put(enc_all, near, enc_half, 0)
        put(dec_all, near, dec_half, 0)
        for table, source in ((FAR_0, first), (FAR_1, second)):
            block = look_up(sender(table), rank)
            put(enc_all, block, source, 0)
            put(dec_all, block, source, strips)

    put(enc_all, rank, own, 0)
    put(dec_all, rank, own, strips)

    @pl.when(core == 0)
    def _():
        unpack(one, one_other, far, far_other)

    @pl.when(core == 1)
    def _():
        unpack(one_other, one, far_other, far)

    bias = sum(source[:, -TILE:].astype(F32) for source in (own, one, far, far_other))[0:1, :]
    bias_col = jnp.broadcast_to(bias, (TILE, TILE)).T
    base = dec_bias[...].reshape(1, width)
    half = pieces[0].shape[1]
    cols = pl.ds(pl.multiple_of((chip ^ core) * half, half), half)
    chunks = []
    for group in (refs[: 2 * parts], refs[2 * parts :]):
        chunks += list(zip(group[:parts], group[parts:], strict=True))
    n = chunks[0][0].shape[0]
    merge = 512 // n
    for i in range(0, len(chunks), merge):
        span = slice(i * n, (i + merge) * n)
        some = chunks[i : i + merge]

        def stack(values):
            return values[0] if len(values) == 1 else jnp.concatenate(values, axis=0)

        x = stack([part[:, :width] for part, _ in some])
        target = stack([part[:, :width] for _, part in some]).astype(F32)
        gate = [part[:, width:] for _, part in some]
        gate = (gate[0] if len(gate) == 1 else jnp.concatenate(gate, axis=1)).astype(F32)
        pre = contract(enc_all[...], x, 1, 1)
        bias_cols = jnp.concatenate([bias_col] * (pre.shape[1] // TILE), axis=1)
        act = ((pre + bias_cols) * gate).astype(BF16)
        recon_full = contract(act, dec_all[...], 0, 0) + base
        if i < parts:
            recon[...] = recon_full[: recon.shape[0]].astype(BF16)
        error = (recon_full - target).astype(BF16)
        error_all[span, :] = error
        act_all[:, span] = act
        dpre_all[:, span] = (contract(dec_all[...], error, 1, 1) * gate).astype(BF16)
        for j, (part, _) in enumerate(some):
            inputs_all[(i + j) * n : (i + j + 1) * n, :] = part[:, cols]
    dec_terms[...] = contract(act_all[...], error_all[:, cols], 1, 0)
    enc_terms[...] = contract(dpre_all[...], inputs_all[...], 1, 0)
    for zero, one_table, piece in zip(CORE_0, CORE_1, pieces, strict=True):
        to = look_up(one_table, rank)
        if zero is not None:
            to = jnp.where(core == 0, look_up(zero, rank), to)
        piece[:rows, :] = enc_terms[at(to), :].astype(BF16)
        piece[rows:, :] = dec_terms[at(to), :].astype(BF16)
    own_piece[:rows, :] = enc_terms[at(rank), :]
    own_piece[rows:, :] = dec_terms[at(rank), :]


def owner_kernel(*refs):
    *arrived, own, send, keep = refs
    share = keep.shape[1]
    core = lax.axis_index("tok") % 2
    total = sum(part[...].astype(F32) for part in arrived)

    @pl.when(core == 0)
    def _():
        whole = total + own[...]
        keep[...] = whole[:, :share]
        send[...] = whole[:, share:].astype(BF16)

    @pl.when(core == 1)
    def _():
        keep[...] = total[:, share:]
        send[...] = total[:, :share].astype(BF16)


def last_kernel(factor, keep, came, grad_enc, grad_dec):
    rows = grad_enc.shape[0]
    total = (keep[...] + came[...].astype(F32)) * factor
    grad_enc[...] = total[:rows]
    grad_dec[...] = total[rows:]


def small_body(inputs, targets, mask, enc_weight, enc_bias, dec_weight, dec_bias):
    blks, toks = lax.axis_size("blk"), lax.axis_size("tok")
    rows, width = enc_weight.shape
    tokens, latents = mask.shape
    share = width // toks
    factor = 1.0 / math.sqrt(tokens * blks * toks)

    def swap(array):
        return move(array, blks, toks, lambda b, t: (b, t ^ 1))

    strips = rows // STRIP
    whole, half = pl.pallas_call(
        pack_kernel,
        out_shape=[
            pltpu.VMEM((STRIP, 2 * strips * width + TILE), BF16),
            pltpu.VMEM((STRIP, strips * width + TILE), BF16),
        ],
        in_specs=[pl.BlockSpec(memory_space=pl.ANY)] * 3,
        out_specs=[VMEM] * 2,
        scratch_shapes=[pltpu.VMEM((rows,), BF16), pltpu.SemaphoreType.DMA((1 + 2 * strips,))],
    )(enc_weight, dec_weight, enc_bias)
    far = move(whole, blks, toks, lambda b, t: ((FAR_0, FAR_1)[t % 2][b], t))
    one = move(half, blks, toks, lambda b, t: (NEAR[b], t))
    parts = 2
    *loaded, dec_bias = pl.pallas_call(
        load_kernel,
        out_shape=[pltpu.VMEM((tokens // parts, width), BF16)] * parts
        + [pltpu.VMEM((tokens // parts, width + latents), BF16)] * parts
        + [pltpu.VMEM(dec_bias.shape, F32)],
        in_specs=[pl.BlockSpec(memory_space=pl.ANY)] * 4 + [VMEM],
        out_specs=[VMEM] * (2 * parts + 1),
        scratch_shapes=[pltpu.VMEM(mask.shape, mask.dtype), pltpu.SemaphoreType.DMA((2 * parts + 2,))],
        cost_estimate=pl.CostEstimate(flops=0, bytes_accessed=4 * tokens * width, transcendentals=0),
    )(inputs, targets, mask, dec_bias, in_vmem(half))
    others = [swap(array) for array in loaded]
    joined = kernel_call(
        join_kernel, [pltpu.VMEM((STRIP, 3 * strips * width + 2 * TILE), BF16)], far, one
    )
    other = swap(*joined)
    piece = (2 * rows, 2 * share)
    recon, *pieces, own = kernel_call(
        step_kernel,
        [pltpu.VMEM((tokens, width), BF16)]
        + [pltpu.VMEM(piece, BF16)] * len(CORE_1)
        + [pltpu.VMEM(piece, F32)],
        dec_bias, whole, one, far, other, *loaded, *others,
        scratch=[
            pltpu.VMEM((latents, width), BF16),
            pltpu.VMEM((latents, width), BF16),
            pltpu.VMEM((2 * tokens, width), BF16),
            pltpu.VMEM((latents, 2 * tokens), BF16),
            pltpu.VMEM((latents, 2 * tokens), BF16),
            pltpu.VMEM((2 * tokens, 2 * share), BF16),
            pltpu.VMEM((latents, 2 * share), F32),
            pltpu.VMEM((latents, 2 * share), F32),
        ],
        flops=16 * tokens * latents * width,
    )
    arrived = []
    for zero, one_table, out in zip(CORE_0, CORE_1, pieces, strict=True):

        def where(b, t, tables=(zero, one_table)):
            table = tables[t % 2]
            return None if table is None else (table[b], t ^ (2 * (t % 2)))

        arrived.append(move(out, blks, toks, where))
    send, keep = kernel_call(
        owner_kernel,
        [pltpu.VMEM((2 * rows, share), BF16), pltpu.VMEM((2 * rows, share), F32)],
        *arrived, own,
    )
    came = swap(send)
    grad_enc, grad_dec = kernel_call(
        lambda *refs: last_kernel(factor, *refs),
        [jax.ShapeDtypeStruct((rows, share), F32)] * 2,
        keep, came,
    )
    return recon, grad_enc, grad_dec


def large_body(inputs, targets, mask, enc_weight, enc_bias, dec_weight, dec_bias):
    gate = mask.astype(F32)
    enc_all = lax.all_gather(enc_weight, "blk", axis=0, tiled=True)
    dec_all = lax.all_gather(dec_weight, "blk", axis=0, tiled=True)
    bias_all = lax.all_gather(enc_bias, "blk", axis=0, tiled=True)
    pre = lax.dot_general(
        inputs, enc_all, (((1,), (1,)), ((), ())), preferred_element_type=F32
    )
    act = ((pre + bias_all.astype(F32)[None, :]) * gate).astype(BF16)
    recon_full = jnp.dot(act, dec_all, preferred_element_type=F32) + dec_bias[None, :]
    error = (recon_full - targets.astype(F32)).astype(BF16)
    back = lax.dot_general(
        error, dec_all, (((1,), (1,)), ((), ())), preferred_element_type=F32
    )
    dpre = (back * gate).astype(BF16)
    total = inputs.shape[0] * lax.axis_size("blk") * lax.axis_size("tok")
    factor = 1.0 / math.sqrt(total)
    grads = []
    for left, right in ((dpre, inputs), (act, error)):
        terms = lax.dot_general(
            left, right, (((0,), (0,)), ((), ())), preferred_element_type=F32
        )
        terms = lax.psum_scatter(terms, "blk", scatter_dimension=0, tiled=True)
        terms = lax.psum_scatter(terms, "tok", scatter_dimension=1, tiled=True)
        grads.append(terms * factor)
    return recon_full.astype(BF16), grads[0], grads[1]


def solution(mesh):
    small = mesh.shape["blk"] == 4 and mesh.shape["tok"] == 4
    tokens = P(("layers", "blk", "tok"), None)
    rows = P(("layers", "blk"), None)
    return jax.shard_map(
        small_body if small else large_body,
        mesh=mesh,
        in_specs=(tokens, tokens, tokens, rows, P(("layers", "blk")), rows, P("layers")),
        out_specs=(tokens, P(("layers", "blk"), "tok"), P(("layers", "blk"), "tok")),
        check_vma=False,
    )
```

```python
import math

import jax
import jax.numpy as jnp
from jax import lax
from jax.experimental import pallas as pl
from jax.experimental.pallas import tpu as pltpu
from jax.sharding import PartitionSpec as P

BF16 = jnp.bfloat16
F32 = jnp.float32
VMEM = pl.BlockSpec(memory_space=pltpu.VMEM)
PAIR = ("blk", "tok")
STRIP = 16
TILE = 128

FAR_0, FAR_1, NEAR = ((3, 2, 1, 0), (2, 3, 0, 1), (1, 0, 3, 2))
CORE_0 = ((2, 3, 0, 1), (3, 2, 1, 0), (1, 0, 3, 2), (0, 1, 2, 3))
CORE_1 = ((1, 3, 0, 2), (3, 2, 1, 0), (2, 0, 3, 1), (0, 1, 2, 3))


def look_up(table, index):
    value = table[-1]
    for i in range(len(table) - 1):
        value = jnp.where(index == i, table[i], value)
    return value


def sender(table):
    return tuple(table.index(i) for i in range(len(table)))


def in_vmem(array):
    return pltpu.with_memory_space_constraint(array, pltpu.VMEM)


def kernel_call(kernel, outs, *operands, scratch=(), flops=0):
    return pl.pallas_call(
        kernel,
        out_shape=outs,
        in_specs=[VMEM] * len(operands),
        out_specs=[VMEM] * len(outs),
        scratch_shapes=list(scratch),
        cost_estimate=pl.CostEstimate(flops=flops, bytes_accessed=0, transcendentals=0),
        compiler_params=pltpu.CompilerParams(vmem_limit_bytes=32 * 1024 * 1024),
    )(*[in_vmem(operand) for operand in operands])


def move(array, blks, toks, where):
    pairs = []
    for b in range(blks):
        for t in range(toks):
            to = where(b, t)
            pairs.append((b * toks + t, to[0] * toks + to[1]))
    return lax.ppermute(array, PAIR, pairs)


def pack_kernel(enc, dec, bias, whole, half, side, sems):
    rows, width = enc.shape
    rank = lax.axis_index("blk")
    core = lax.axis_index("tok") % 2
    strips = rows // STRIP
    copies = [pltpu.make_async_copy(bias, side, sems.at[0])]
    for k, source in enumerate((enc, dec)):
        for i in range(strips):
            j = k * strips + i
            copies.append(
                pltpu.make_async_copy(
                    source.at[pl.ds(i * STRIP, STRIP)], whole.at[:, pl.ds(j * width, width)], sems.at[1 + j]
                )
            )
    for copy in copies:
        copy.start()
    copies[0].wait()
    tile = jnp.broadcast_to(side[...].astype(F32).reshape(1, rows), (STRIP, rows))
    tile = jnp.concatenate([tile, jnp.zeros((STRIP, TILE - rows), F32)], axis=1)
    tile = pltpu.roll(tile, rank * rows, axis=1).astype(BF16)
    whole[:, 2 * strips * width :] = tile
    half[:, strips * width :] = tile
    for copy in copies[1:]:
        copy.wait()

    @pl.when(core == 0)
    def _():
        half[:, : strips * width] = whole[:, : strips * width]

    @pl.when(core == 1)
    def _():
        half[:, : strips * width] = whole[:, strips * width : 2 * strips * width]


def load_kernel(inputs, targets, mask, dec_bias, after, *refs):
    *outs, dec_bias_out, mask_ints, sems = refs
    parts = len(outs) // 2
    width = inputs.shape[1]
    copies = [(mask, mask_ints), (dec_bias, dec_bias_out)]
    for i, source in enumerate((inputs, targets)):
        for j, out in enumerate(outs[i * parts : (i + 1) * parts]):
            rows = out.shape[0]
            copies.append((source.at[pl.ds(j * rows, rows)], out.at[:, pl.ds(0, width)]))
    copies = [pltpu.make_async_copy(*pair, sems.at[i]) for i, pair in enumerate(copies)]
    for copy in copies:
        copy.start()
    copies[0].wait()
    for j, out in enumerate(outs[parts:]):
        rows = out.shape[0]
        out[:, width:] = mask_ints[j * rows : (j + 1) * rows, :].astype(F32).T.astype(BF16)
    for copy in copies[1:]:
        copy.wait()


def join_kernel(far, one, out):
    out[:, : far.shape[1]] = far[...]
    out[:, far.shape[1] :] = one[...]


def contract(a, b, over_a, over_b):
    return lax.dot_general(a, b, (((over_a,), (over_b,)), ((), ())), preferred_element_type=F32)


def step_kernel(dec_bias, own, one, far, other, *refs):
    *refs, enc_all, dec_all, error_all, act_all, dpre_all, inputs_all, enc_terms, dec_terms = refs
    *refs, own_piece = refs
    refs, pieces = refs[: -len(CORE_1)], refs[-len(CORE_1) :]
    *refs, recon = refs
    parts = len(refs) // 4
    width = recon.shape[1]
    strips = one.shape[1] // width
    rows = strips * STRIP
    far_other = other.at[:, pl.ds(0, far.shape[1])]
    one_other = other.at[:, pl.ds(far.shape[1], one.shape[1])]
    rank = lax.axis_index("blk")
    tok = lax.axis_index("tok")
    core = tok % 2
    chip = tok // 2

    def at(block):
        return pl.ds(pl.multiple_of(block * rows, rows), rows)

    def put(to, block, source, first):
        for i in range(strips):
            span = pl.ds(pl.multiple_of(block * rows + i * STRIP, STRIP), STRIP)
            j = first + i
            to[span, :] = source[:, j * width : (j + 1) * width]

    def unpack(enc_half, dec_half, first, second):
        near = look_up(sender(NEAR), rank)
        put(enc_all, near, enc_half, 0)
        put(dec_all, near, dec_half, 0)
        for table, source in ((FAR_0, first), (FAR_1, second)):
            block = look_up(sender(table), rank)
            put(enc_all, block, source, 0)
            put(dec_all, block, source, strips)

    put(enc_all, rank, own, 0)
    put(dec_all, rank, own, strips)

    @pl.when(core == 0)
    def _():
        unpack(one, one_other, far, far_other)

    @pl.when(core == 1)
    def _():
        unpack(one_other, one, far_other, far)

    bias = sum(source[:, -TILE:].astype(F32) for source in (own, one, far, far_other))[0:1, :]
    bias_col = jnp.broadcast_to(bias, (TILE, TILE)).T
    base = dec_bias[...].reshape(1, width)
    half = pieces[0].shape[1]
    cols = pl.ds(pl.multiple_of((chip ^ core) * half, half), half)
    input_parts = (*refs[:parts], *refs[2 * parts : 3 * parts])
    target_parts = (*refs[parts : 2 * parts], *refs[3 * parts :])
    x = jnp.concatenate([part[...] for part in input_parts], axis=0)
    target = jnp.concatenate([part[:, :width] for part in target_parts], axis=0).astype(F32)
    gate = jnp.concatenate([part[:, width:] for part in target_parts], axis=1).astype(F32)
    pre = contract(enc_all[...], x, 1, 1)
    pre = pre + jnp.concatenate([bias_col] * (pre.shape[1] // TILE), axis=1)
    act = (pre * gate).astype(BF16)
    recon_full = contract(act, dec_all[...], 0, 0) + base
    recon[...] = recon_full[: recon.shape[0]].astype(BF16)
    error = (recon_full - target).astype(BF16)
    error_all[...] = error
    act_all[...] = act
    dpre_all[...] = (contract(dec_all[...], error, 1, 1) * gate).astype(BF16)
    n = input_parts[0].shape[0]
    for i, part in enumerate(input_parts):
        inputs_all[i * n : (i + 1) * n, :] = part[:, cols]
    dec_terms[...] = contract(act_all[...], error_all[:, cols], 1, 0)
    enc_terms[...] = contract(dpre_all[...], inputs_all[...], 1, 0)
    for zero, one_table, piece in zip(CORE_0, CORE_1, pieces, strict=True):
        to = jnp.where(core == 0, look_up(zero, rank), look_up(one_table, rank))
        piece[:rows, :] = enc_terms[at(to), :].astype(BF16)
        piece[rows:, :] = dec_terms[at(to), :].astype(BF16)
    own_piece[:rows, :] = enc_terms[at(rank), :]
    own_piece[rows:, :] = dec_terms[at(rank), :]


def owner_kernel(*refs):
    *arrived, own, send, keep = refs
    share = keep.shape[1]
    core = lax.axis_index("tok") % 2
    total = sum(part[...].astype(F32) for part in arrived[:-1])

    @pl.when(core == 0)
    def _():
        whole = total + own[...]
        keep[...] = whole[:, :share]
        send[...] = whole[:, share:].astype(BF16)

    @pl.when(core == 1)
    def _():
        whole = total + arrived[-1][...].astype(F32)
        keep[...] = whole[:, share:]
        send[...] = whole[:, :share].astype(BF16)


def last_kernel(factor, keep, came, grad_enc, grad_dec):
    rows = grad_enc.shape[0]
    total = (keep[...] + came[...].astype(F32)) * factor
    grad_enc[...] = total[:rows]
    grad_dec[...] = total[rows:]


def small_body(inputs, targets, mask, enc_weight, enc_bias, dec_weight, dec_bias):
    blks, toks = lax.axis_size("blk"), lax.axis_size("tok")
    rows, width = enc_weight.shape
    tokens, latents = mask.shape
    share = width // toks
    factor = 1.0 / math.sqrt(tokens * blks * toks)

    def swap(array):
        return move(array, blks, toks, lambda b, t: (b, t ^ 1))

    strips = rows // STRIP
    whole, half = pl.pallas_call(
        pack_kernel,
        out_shape=[
            pltpu.VMEM((STRIP, 2 * strips * width + TILE), BF16),
            pltpu.VMEM((STRIP, strips * width + TILE), BF16),
        ],
        in_specs=[pl.BlockSpec(memory_space=pl.ANY)] * 3,
        out_specs=[VMEM] * 2,
        scratch_shapes=[pltpu.VMEM((rows,), BF16), pltpu.SemaphoreType.DMA((1 + 2 * strips,))],
    )(enc_weight, dec_weight, enc_bias)
    far = move(whole, blks, toks, lambda b, t: ((FAR_0, FAR_1)[t % 2][b], t))
    one = move(half, blks, toks, lambda b, t: (NEAR[b], t))
    parts = 2
    *loaded, dec_bias = pl.pallas_call(
        load_kernel,
        out_shape=[pltpu.VMEM((tokens // parts, width), BF16)] * parts
        + [pltpu.VMEM((tokens // parts, width + latents), BF16)] * parts
        + [pltpu.VMEM(dec_bias.shape, F32)],
        in_specs=[pl.BlockSpec(memory_space=pl.ANY)] * 4 + [VMEM],
        out_specs=[VMEM] * (2 * parts + 1),
        scratch_shapes=[pltpu.VMEM(mask.shape, mask.dtype), pltpu.SemaphoreType.DMA((2 * parts + 2,))],
        cost_estimate=pl.CostEstimate(flops=0, bytes_accessed=4 * tokens * width, transcendentals=0),
    )(inputs, targets, mask, dec_bias, in_vmem(half))
    others = [swap(array) for array in loaded]
    joined = kernel_call(
        join_kernel, [pltpu.VMEM((STRIP, 3 * strips * width + 2 * TILE), BF16)], far, one
    )
    other = swap(*joined)
    piece = (2 * rows, 2 * share)
    recon, *pieces, own = kernel_call(
        step_kernel,
        [pltpu.VMEM((tokens, width), BF16)]
        + [pltpu.VMEM(piece, BF16)] * len(CORE_1)
        + [pltpu.VMEM(piece, F32)],
        dec_bias, whole, one, far, other, *loaded, *others,
        scratch=[
            pltpu.VMEM((latents, width), BF16),
            pltpu.VMEM((latents, width), BF16),
            pltpu.VMEM((2 * tokens, width), BF16),
            pltpu.VMEM((latents, 2 * tokens), BF16),
            pltpu.VMEM((latents, 2 * tokens), BF16),
            pltpu.VMEM((2 * tokens, 2 * share), BF16),
            pltpu.VMEM((latents, 2 * share), F32),
            pltpu.VMEM((latents, 2 * share), F32),
        ],
        flops=16 * tokens * latents * width,
    )
    arrived = []
    for zero, one_table, out in zip(CORE_0, CORE_1, pieces, strict=True):

        def where(b, t, tables=(zero, one_table)):
            to = tables[t % 2][b]
            return (to, t ^ 2 if t % 2 or to == b else t)

        arrived.append(move(out, blks, toks, where))
    send, keep = kernel_call(
        owner_kernel,
        [pltpu.VMEM((2 * rows, share), BF16), pltpu.VMEM((2 * rows, share), F32)],
        *arrived, own,
    )
    came = swap(send)
    grad_enc, grad_dec = kernel_call(
        lambda *refs: last_kernel(factor, *refs),
        [jax.ShapeDtypeStruct((rows, share), F32)] * 2,
        keep, came,
    )
    return recon, grad_enc, grad_dec


def large_body(inputs, targets, mask, enc_weight, enc_bias, dec_weight, dec_bias):
    gate = mask.astype(F32)
    enc_all = lax.all_gather(enc_weight, "blk", axis=0, tiled=True)
    dec_all = lax.all_gather(dec_weight, "blk", axis=0, tiled=True)
    bias_all = lax.all_gather(enc_bias, "blk", axis=0, tiled=True)
    pre = lax.dot_general(
        inputs, enc_all, (((1,), (1,)), ((), ())), preferred_element_type=F32
    )
    act = ((pre + bias_all.astype(F32)[None, :]) * gate).astype(BF16)
    recon_full = jnp.dot(act, dec_all, preferred_element_type=F32) + dec_bias[None, :]
    error = (recon_full - targets.astype(F32)).astype(BF16)
    back = lax.dot_general(
        error, dec_all, (((1,), (1,)), ((), ())), preferred_element_type=F32
    )
    dpre = (back * gate).astype(BF16)
    total = inputs.shape[0] * lax.axis_size("blk") * lax.axis_size("tok")
    factor = 1.0 / math.sqrt(total)
    grads = []
    for left, right in ((dpre, inputs), (act, error)):
        terms = lax.dot_general(
            left, right, (((0,), (0,)), ((), ())), preferred_element_type=F32
        )
        terms = lax.psum_scatter(terms, "blk", scatter_dimension=0, tiled=True)
        terms = lax.psum_scatter(terms, "tok", scatter_dimension=1, tiled=True)
        grads.append(terms * factor)
    return recon_full.astype(BF16), grads[0], grads[1]


def solution(mesh):
    small = mesh.shape["blk"] == 4 and mesh.shape["tok"] == 4
    tokens = P(("layers", "blk", "tok"), None)
    rows = P(("layers", "blk"), None)
    return jax.shard_map(
        small_body if small else large_body,
        mesh=mesh,
        in_specs=(tokens, tokens, tokens, rows, P(("layers", "blk")), rows, P("layers")),
        out_specs=(tokens, P(("layers", "blk"), "tok"), P(("layers", "blk"), "tok")),
        check_vma=False,
    )
```

```python
import math

import jax
import jax.numpy as jnp
from jax import lax
from jax.experimental import pallas as pl
from jax.experimental.pallas import tpu as pltpu
from jax.sharding import PartitionSpec as P

BF16 = jnp.bfloat16
F32 = jnp.float32
VMEM = pl.BlockSpec(memory_space=pltpu.VMEM)
PAIR = ("blk", "tok")
STRIP = 16
TILE = 128

FAR_0, FAR_1, NEAR = ((3, 2, 1, 0), (2, 3, 0, 1), (1, 0, 3, 2))
CORE_0 = ((2, 3, 0, 1), (3, 2, 1, 0), (1, 0, 3, 2), (0, 1, 2, 3))
CORE_1 = ((1, 3, 0, 2), (3, 2, 1, 0), (2, 0, 3, 1), (0, 1, 2, 3))


def look_up(table, index):
    value = table[-1]
    for i in range(len(table) - 1):
        value = jnp.where(index == i, table[i], value)
    return value


def sender(table):
    return tuple(table.index(i) for i in range(len(table)))


def in_vmem(array):
    return pltpu.with_memory_space_constraint(array, pltpu.VMEM)


def kernel_call(kernel, outs, *operands, scratch=(), flops=0):
    return pl.pallas_call(
        kernel,
        out_shape=outs,
        in_specs=[VMEM] * len(operands),
        out_specs=[VMEM] * len(outs),
        scratch_shapes=list(scratch),
        cost_estimate=pl.CostEstimate(flops=flops, bytes_accessed=0, transcendentals=0),
        compiler_params=pltpu.CompilerParams(vmem_limit_bytes=32 * 1024 * 1024),
    )(*[in_vmem(operand) for operand in operands])


def move(array, blks, toks, where):
    pairs = []
    for b in range(blks):
        for t in range(toks):
            to = where(b, t)
            pairs.append((b * toks + t, to[0] * toks + to[1]))
    return lax.ppermute(array, PAIR, pairs)


def pack_kernel(enc, dec, bias, whole, side, sems):
    rows, width = enc.shape
    rank = lax.axis_index("blk")
    strips = rows // STRIP
    copies = [pltpu.make_async_copy(bias, side, sems.at[0])]
    for k, source in enumerate((enc, dec)):
        for i in range(strips):
            j = k * strips + i
            copies.append(
                pltpu.make_async_copy(
                    source.at[pl.ds(i * STRIP, STRIP)], whole.at[:, pl.ds(j * width, width)], sems.at[1 + j]
                )
            )
    for copy in copies:
        copy.start()
    copies[0].wait()
    tile = jnp.broadcast_to(side[...].astype(F32).reshape(1, rows), (STRIP, rows))
    tile = jnp.concatenate([tile, jnp.zeros((STRIP, TILE - rows), F32)], axis=1)
    tile = pltpu.roll(tile, rank * rows, axis=1).astype(BF16)
    whole[:, 2 * strips * width :] = tile
    for copy in copies[1:]:
        copy.wait()


def half_kernel(whole, half):
    core = lax.axis_index("tok") % 2
    size = half.shape[1] - TILE

    @pl.when(core == 0)
    def _():
        half[:, :size] = whole[:, :size]

    @pl.when(core == 1)
    def _():
        half[:, :size] = whole[:, size : 2 * size]

    half[:, size:] = whole[:, 2 * size :]


def load_kernel(inputs, targets, mask, dec_bias, after, *refs):
    *outs, dec_bias_out, mask_ints, sems = refs
    parts = len(outs) // 2
    width = inputs.shape[1]
    copies = [(mask, mask_ints), (dec_bias, dec_bias_out)]
    for i, source in enumerate((inputs, targets)):
        for j, out in enumerate(outs[i * parts : (i + 1) * parts]):
            rows = out.shape[0]
            copies.append((source.at[pl.ds(j * rows, rows)], out.at[:, pl.ds(0, width)]))
    copies = [pltpu.make_async_copy(*pair, sems.at[i]) for i, pair in enumerate(copies)]
    for copy in copies:
        copy.start()
    copies[0].wait()
    for j, out in enumerate(outs[parts:]):
        rows = out.shape[0]
        out[:, width:] = mask_ints[j * rows : (j + 1) * rows, :].astype(F32).T.astype(BF16)
    for copy in copies[1:]:
        copy.wait()


def join_kernel(far, one, out):
    out[:, : far.shape[1]] = far[...]
    out[:, far.shape[1] :] = one[...]


def contract(a, b, over_a, over_b):
    return lax.dot_general(a, b, (((over_a,), (over_b,)), ((), ())), preferred_element_type=F32)


def step_kernel(dec_bias, own, one, far, other, *refs):
    *refs, enc_all, dec_all, error_all, dpre_all, inputs_all, enc_terms, dec_terms = refs
    *refs, own_piece = refs
    refs, pieces = refs[: -len(CORE_1)], refs[-len(CORE_1) :]
    *refs, recon = refs
    parts = len(refs) // 4
    width = recon.shape[1]
    strips = one.shape[1] // width
    rows = strips * STRIP
    far_other = other.at[:, pl.ds(0, far.shape[1])]
    one_other = other.at[:, pl.ds(far.shape[1], one.shape[1])]
    rank = lax.axis_index("blk")
    tok = lax.axis_index("tok")
    core = tok % 2
    chip = tok // 2

    def at(block):
        return pl.ds(pl.multiple_of(block * rows, rows), rows)

    def put(to, block, source, first):
        for i in range(strips):
            span = pl.ds(pl.multiple_of(block * rows + i * STRIP, STRIP), STRIP)
            j = first + i
            to[span, :] = source[:, j * width : (j + 1) * width]

    def unpack(enc_half, dec_half, first, second):
        near = look_up(sender(NEAR), rank)
        put(enc_all, near, enc_half, 0)
        put(dec_all, near, dec_half, 0)
        for table, source in ((FAR_0, first), (FAR_1, second)):
            block = look_up(sender(table), rank)
            put(enc_all, block, source, 0)
            put(dec_all, block, source, strips)

    put(enc_all, rank, own, 0)
    put(dec_all, rank, own, strips)

    @pl.when(core == 0)
    def _():
        unpack(one, one_other, far, far_other)

    @pl.when(core == 1)
    def _():
        unpack(one_other, one, far_other, far)

    bias = sum(source[:, -TILE:].astype(F32) for source in (own, one, far, far_other))[0:1, :]
    bias_col = jnp.broadcast_to(bias, (TILE, TILE)).T
    base = dec_bias[...].reshape(1, width)
    half = pieces[0].shape[1]
    cols = pl.ds(pl.multiple_of((chip ^ core) * half, half), half)
    input_parts = (*refs[:parts], *refs[2 * parts : 3 * parts])
    target_parts = (*refs[parts : 2 * parts], *refs[3 * parts :])
    x = jnp.concatenate([part[...] for part in input_parts], axis=0)
    target = jnp.concatenate([part[:, :width] for part in target_parts], axis=0).astype(F32)
    gate = jnp.concatenate([part[:, width:] for part in target_parts], axis=1).astype(F32)
    pre = contract(enc_all[...], x, 1, 1)
    pre = pre + jnp.concatenate([bias_col] * (pre.shape[1] // TILE), axis=1)
    act = (pre * gate).astype(BF16)
    recon_full = contract(act, dec_all[...], 0, 0) + base
    recon[...] = recon_full[: recon.shape[0]].astype(BF16)
    error = (recon_full - target).astype(BF16)
    error_all[...] = error
    dpre_all[...] = (contract(dec_all[...], error, 1, 1) * gate).astype(BF16)
    n = input_parts[0].shape[0]
    for i, part in enumerate(input_parts):
        inputs_all[i * n : (i + 1) * n, :] = part[:, cols]
    dec_terms[...] = contract(act, error_all[:, cols], 1, 0)
    enc_terms[...] = contract(dpre_all[...], inputs_all[...], 1, 0)
    for zero, one_table, piece in zip(CORE_0, CORE_1, pieces, strict=True):
        to = jnp.where(core == 0, look_up(zero, rank), look_up(one_table, rank))
        piece[:rows, :] = enc_terms[at(to), :].astype(BF16)
        piece[rows:, :] = dec_terms[at(to), :].astype(BF16)
    own_piece[:rows, :] = enc_terms[at(rank), :]
    own_piece[rows:, :] = dec_terms[at(rank), :]


def owner_kernel(*refs):
    *arrived, own, send, keep = refs
    share = keep.shape[1]
    core = lax.axis_index("tok") % 2
    total = sum(part[...].astype(F32) for part in arrived[:-1])

    @pl.when(core == 0)
    def _():
        whole = total + own[...]
        keep[...] = whole[:, :share]
        send[...] = whole[:, share:].astype(BF16)

    @pl.when(core == 1)
    def _():
        whole = total + arrived[-1][...].astype(F32)
        keep[...] = whole[:, share:]
        send[...] = whole[:, :share].astype(BF16)


def last_kernel(factor, keep, came, grad_enc, grad_dec):
    rows = grad_enc.shape[0]
    total = (keep[...] + came[...].astype(F32)) * factor
    grad_enc[...] = total[:rows]
    grad_dec[...] = total[rows:]


def small_body(inputs, targets, mask, enc_weight, enc_bias, dec_weight, dec_bias):
    blks, toks = lax.axis_size("blk"), lax.axis_size("tok")
    rows, width = enc_weight.shape
    tokens, latents = mask.shape
    share = width // toks
    factor = 1.0 / math.sqrt(tokens * blks * toks)

    def swap(array):
        return move(array, blks, toks, lambda b, t: (b, t ^ 1))

    strips = rows // STRIP
    whole = pl.pallas_call(
        pack_kernel,
        out_shape=pltpu.VMEM((STRIP, 2 * strips * width + TILE), BF16),
        in_specs=[pl.BlockSpec(memory_space=pl.ANY)] * 3,
        out_specs=VMEM,
        scratch_shapes=[pltpu.VMEM((rows,), BF16), pltpu.SemaphoreType.DMA((1 + 2 * strips,))],
    )(enc_weight, dec_weight, enc_bias)
    far = move(whole, blks, toks, lambda b, t: ((FAR_0, FAR_1)[t % 2][b], t))
    (half,) = kernel_call(half_kernel, [pltpu.VMEM((STRIP, strips * width + TILE), BF16)], whole)
    one = move(half, blks, toks, lambda b, t: (NEAR[b], t))
    parts = 2
    *loaded, dec_bias = pl.pallas_call(
        load_kernel,
        out_shape=[pltpu.VMEM((tokens // parts, width), BF16)] * parts
        + [pltpu.VMEM((tokens // parts, width + latents), BF16)] * parts
        + [pltpu.VMEM(dec_bias.shape, F32)],
        in_specs=[pl.BlockSpec(memory_space=pl.ANY)] * 4 + [VMEM],
        out_specs=[VMEM] * (2 * parts + 1),
        scratch_shapes=[pltpu.VMEM(mask.shape, mask.dtype), pltpu.SemaphoreType.DMA((2 * parts + 2,))],
        cost_estimate=pl.CostEstimate(flops=0, bytes_accessed=4 * tokens * width, transcendentals=0),
    )(inputs, targets, mask, dec_bias, in_vmem(half))
    others = [swap(array) for array in loaded]
    joined = kernel_call(
        join_kernel, [pltpu.VMEM((STRIP, 3 * strips * width + 2 * TILE), BF16)], far, one
    )
    other = swap(*joined)
    piece = (2 * rows, 2 * share)
    recon, *pieces, own = kernel_call(
        step_kernel,
        [pltpu.VMEM((tokens, width), BF16)]
        + [pltpu.VMEM(piece, BF16)] * len(CORE_1)
        + [pltpu.VMEM(piece, F32)],
        dec_bias, whole, one, far, other, *loaded, *others,
        scratch=[
            pltpu.VMEM((latents, width), BF16),
            pltpu.VMEM((latents, width), BF16),
            pltpu.VMEM((2 * tokens, width), BF16),
            pltpu.VMEM((latents, 2 * tokens), BF16),
            pltpu.VMEM((2 * tokens, 2 * share), BF16),
            pltpu.VMEM((latents, 2 * share), F32),
            pltpu.VMEM((latents, 2 * share), F32),
        ],
        flops=16 * tokens * latents * width,
    )
    arrived = []
    for zero, one_table, out in zip(CORE_0, CORE_1, pieces, strict=True):

        def where(b, t, tables=(zero, one_table)):
            to = tables[t % 2][b]
            return (to, t ^ 2 if t % 2 or to == b else t)

        arrived.append(move(out, blks, toks, where))
    send, keep = kernel_call(
        owner_kernel,
        [pltpu.VMEM((2 * rows, share), BF16), pltpu.VMEM((2 * rows, share), F32)],
        *arrived, own,
    )
    came = swap(send)
    grad_enc, grad_dec = kernel_call(
        lambda *refs: last_kernel(factor, *refs),
        [jax.ShapeDtypeStruct((rows, share), F32)] * 2,
        keep, came,
    )
    return recon, grad_enc, grad_dec


def large_body(inputs, targets, mask, enc_weight, enc_bias, dec_weight, dec_bias):
    gate = mask.astype(F32)
    enc_all = lax.all_gather(enc_weight, "blk", axis=0, tiled=True)
    dec_all = lax.all_gather(dec_weight, "blk", axis=0, tiled=True)
    bias_all = lax.all_gather(enc_bias, "blk", axis=0, tiled=True)
    pre = lax.dot_general(
        inputs, enc_all, (((1,), (1,)), ((), ())), preferred_element_type=F32
    )
    act = ((pre + bias_all.astype(F32)[None, :]) * gate).astype(BF16)
    recon_full = jnp.dot(act, dec_all, preferred_element_type=F32) + dec_bias[None, :]
    error = (recon_full - targets.astype(F32)).astype(BF16)
    back = lax.dot_general(
        error, dec_all, (((1,), (1,)), ((), ())), preferred_element_type=F32
    )
    dpre = (back * gate).astype(BF16)
    total = inputs.shape[0] * lax.axis_size("blk") * lax.axis_size("tok")
    factor = 1.0 / math.sqrt(total)
    grads = []
    for left, right in ((dpre, inputs), (act, error)):
        terms = lax.dot_general(
            left, right, (((0,), (0,)), ((), ())), preferred_element_type=F32
        )
        terms = lax.psum_scatter(terms, "blk", scatter_dimension=0, tiled=True)
        terms = lax.psum_scatter(terms, "tok", scatter_dimension=1, tiled=True)
        grads.append(terms * factor)
    return recon_full.astype(BF16), grads[0], grads[1]


def solution(mesh):
    small = mesh.shape["blk"] == 4 and mesh.shape["tok"] == 4
    tokens = P(("layers", "blk", "tok"), None)
    rows = P(("layers", "blk"), None)
    return jax.shard_map(
        small_body if small else large_body,
        mesh=mesh,
        in_specs=(tokens, tokens, tokens, rows, P(("layers", "blk")), rows, P("layers")),
        out_specs=(tokens, P(("layers", "blk"), "tok"), P(("layers", "blk"), "tok")),
        check_vma=False,
    )
```

```python
import math

import jax
import jax.numpy as jnp
from jax import lax
from jax.experimental import pallas as pl
from jax.experimental.pallas import tpu as pltpu
from jax.sharding import PartitionSpec as P

BF16 = jnp.bfloat16
F32 = jnp.float32
VMEM = pl.BlockSpec(memory_space=pltpu.VMEM)
PAIR = ("blk", "tok")
STRIP = 16
TILE = 128

FAR_0, FAR_1, NEAR = ((3, 2, 1, 0), (2, 3, 0, 1), (1, 0, 3, 2))
CORE_0 = ((2, 3, 0, 1), (3, 2, 1, 0), (1, 0, 3, 2), (0, 1, 2, 3))
CORE_1 = ((1, 3, 0, 2), (3, 2, 1, 0), (2, 0, 3, 1), (0, 1, 2, 3))


def look_up(table, index):
    value = table[-1]
    for i in range(len(table) - 1):
        value = jnp.where(index == i, table[i], value)
    return value


def sender(table):
    return tuple(table.index(i) for i in range(len(table)))


def in_vmem(array):
    return pltpu.with_memory_space_constraint(array, pltpu.VMEM)


def kernel_call(kernel, outs, *operands, scratch=(), flops=0):
    return pl.pallas_call(
        kernel,
        out_shape=outs,
        in_specs=[VMEM] * len(operands),
        out_specs=[VMEM] * len(outs),
        scratch_shapes=list(scratch),
        cost_estimate=pl.CostEstimate(flops=flops, bytes_accessed=0, transcendentals=0),
        compiler_params=pltpu.CompilerParams(vmem_limit_bytes=32 * 1024 * 1024),
    )(*[in_vmem(operand) for operand in operands])


def move(array, blks, toks, where):
    pairs = []
    for b in range(blks):
        for t in range(toks):
            to = where(b, t)
            pairs.append((b * toks + t, to[0] * toks + to[1]))
    return lax.ppermute(array, PAIR, pairs)


def pack_kernel(enc, dec, bias, whole, side, sems):
    rows, width = enc.shape
    rank = lax.axis_index("blk")
    strips = rows // STRIP
    copies = [pltpu.make_async_copy(bias, side, sems.at[0])]
    for k, source in enumerate((enc, dec)):
        for i in range(strips):
            j = k * strips + i
            copies.append(
                pltpu.make_async_copy(
                    source.at[pl.ds(i * STRIP, STRIP)], whole.at[:, pl.ds(j * width, width)], sems.at[1 + j]
                )
            )
    for copy in copies:
        copy.start()
    copies[0].wait()
    tile = jnp.broadcast_to(side[...].astype(F32).reshape(1, rows), (STRIP, rows))
    tile = jnp.concatenate([tile, jnp.zeros((STRIP, TILE - rows), F32)], axis=1)
    tile = pltpu.roll(tile, rank * rows, axis=1).astype(BF16)
    whole[:, 2 * strips * width :] = tile
    for copy in copies[1:]:
        copy.wait()


def half_kernel(whole, half):
    core = lax.axis_index("tok") % 2
    size = half.shape[1] - TILE

    @pl.when(core == 0)
    def _():
        half[:, :size] = whole[:, :size]

    @pl.when(core == 1)
    def _():
        half[:, :size] = whole[:, size : 2 * size]

    half[:, size:] = whole[:, 2 * size :]


def load_kernel(inputs, targets, mask, dec_bias, after, *refs):
    *outs, dec_bias_out, mask_ints, sems = refs
    parts = len(outs) // 2
    width = inputs.shape[1]
    copies = [(mask, mask_ints), (dec_bias, dec_bias_out)]
    for i, source in enumerate((inputs, targets)):
        for j, out in enumerate(outs[i * parts : (i + 1) * parts]):
            rows = out.shape[0]
            copies.append((source.at[pl.ds(j * rows, rows)], out.at[:, pl.ds(0, width)]))
    copies = [pltpu.make_async_copy(*pair, sems.at[i]) for i, pair in enumerate(copies)]
    for copy in copies:
        copy.start()
    copies[0].wait()
    for j, out in enumerate(outs[parts:]):
        rows = out.shape[0]
        out[:, width:] = mask_ints[j * rows : (j + 1) * rows, :].astype(F32).T.astype(BF16)
    for copy in copies[1:]:
        copy.wait()


def join_kernel(far, one, out):
    out[:, : far.shape[1]] = far[...]
    out[:, far.shape[1] :] = one[...]


def contract(a, b, over_a, over_b):
    return lax.dot_general(a, b, (((over_a,), (over_b,)), ((), ())), preferred_element_type=F32)


def step_kernel(dec_bias, own, one, far, other, *refs):
    *refs, enc_all, dec_all, error_all, dpre_all, tokens_all, enc_terms, dec_terms = refs
    *refs, own_piece = refs
    refs, pieces = refs[: -len(CORE_1)], refs[-len(CORE_1) :]
    *refs, recon = refs
    parts = len(refs) // 4
    width = recon.shape[1]
    strips = one.shape[1] // width
    rows = strips * STRIP
    far_other = other.at[:, pl.ds(0, far.shape[1])]
    one_other = other.at[:, pl.ds(far.shape[1], one.shape[1])]
    rank = lax.axis_index("blk")
    tok = lax.axis_index("tok")
    core = tok % 2
    chip = tok // 2

    def at(block):
        return pl.ds(pl.multiple_of(block * rows, rows), rows)

    def put(to, block, source, first):
        for i in range(strips):
            span = pl.ds(pl.multiple_of(block * rows + i * STRIP, STRIP), STRIP)
            j = first + i
            to[span, :] = source[:, j * width : (j + 1) * width]

    def unpack(enc_half, dec_half, first, second):
        near = look_up(sender(NEAR), rank)
        put(enc_all, near, enc_half, 0)
        put(dec_all, near, dec_half, 0)
        for table, source in ((FAR_0, first), (FAR_1, second)):
            block = look_up(sender(table), rank)
            put(enc_all, block, source, 0)
            put(dec_all, block, source, strips)

    put(enc_all, rank, own, 0)
    put(dec_all, rank, own, strips)

    @pl.when(core == 0)
    def _():
        unpack(one, one_other, far, far_other)

    @pl.when(core == 1)
    def _():
        unpack(one_other, one, far_other, far)

    bias = sum(source[:, -TILE:].astype(F32) for source in (own, one, far, far_other))[0:1, :]
    bias_col = jnp.broadcast_to(bias, (TILE, TILE)).T
    base = dec_bias[...].reshape(1, width)
    half = pieces[0].shape[1]
    cols = pl.ds(pl.multiple_of((chip ^ core) * half, half), half)
    input_parts = (*refs[:parts], *refs[2 * parts : 3 * parts])
    target_parts = (*refs[parts : 2 * parts], *refs[3 * parts :])
    n = input_parts[0].shape[0]
    for i, part in enumerate(input_parts):
        tokens_all[i * n : (i + 1) * n, :] = part[...]
    target = jnp.concatenate([part[:, :width] for part in target_parts], axis=0).astype(F32)
    gate = jnp.concatenate([part[:, width:] for part in target_parts], axis=1).astype(F32)
    pre = contract(enc_all[...], tokens_all[...], 1, 1)
    pre = pre + jnp.concatenate([bias_col] * (pre.shape[1] // TILE), axis=1)
    act = (pre * gate).astype(BF16)
    recon_full = contract(act, dec_all[...], 0, 0) + base
    recon[...] = recon_full[: recon.shape[0]].astype(BF16)
    error = (recon_full - target).astype(BF16)
    error_all[...] = error
    dpre_all[...] = (contract(dec_all[...], error, 1, 1) * gate).astype(BF16)
    dec_terms[...] = contract(act, error_all[:, cols], 1, 0)
    enc_terms[...] = contract(dpre_all[...], tokens_all[:, cols], 1, 0)
    for zero, one_table, piece in zip(CORE_0, CORE_1, pieces, strict=True):
        to = jnp.where(core == 0, look_up(zero, rank), look_up(one_table, rank))
        piece[:rows, :] = enc_terms[at(to), :].astype(BF16)
        piece[rows:, :] = dec_terms[at(to), :].astype(BF16)
    own_piece[:rows, :] = enc_terms[at(rank), :]
    own_piece[rows:, :] = dec_terms[at(rank), :]


def owner_kernel(*refs):
    *arrived, own, send, keep = refs
    share = keep.shape[1]
    core = lax.axis_index("tok") % 2
    total = sum(part[...].astype(F32) for part in arrived[:-1])

    @pl.when(core == 0)
    def _():
        whole = total + own[...]
        keep[...] = whole[:, :share]
        send[...] = whole[:, share:].astype(BF16)

    @pl.when(core == 1)
    def _():
        whole = total + arrived[-1][...].astype(F32)
        keep[...] = whole[:, share:]
        send[...] = whole[:, :share].astype(BF16)


def last_kernel(factor, keep, came, grad_enc, grad_dec):
    rows = grad_enc.shape[0]
    total = (keep[...] + came[...].astype(F32)) * factor
    grad_enc[...] = total[:rows]
    grad_dec[...] = total[rows:]


def small_body(inputs, targets, mask, enc_weight, enc_bias, dec_weight, dec_bias):
    blks, toks = lax.axis_size("blk"), lax.axis_size("tok")
    rows, width = enc_weight.shape
    tokens, latents = mask.shape
    share = width // toks
    factor = 1.0 / math.sqrt(tokens * blks * toks)

    def swap(array):
        return move(array, blks, toks, lambda b, t: (b, t ^ 1))

    strips = rows // STRIP
    whole = pl.pallas_call(
        pack_kernel,
        out_shape=pltpu.VMEM((STRIP, 2 * strips * width + TILE), BF16),
        in_specs=[pl.BlockSpec(memory_space=pl.ANY)] * 3,
        out_specs=VMEM,
        scratch_shapes=[pltpu.VMEM((rows,), BF16), pltpu.SemaphoreType.DMA((1 + 2 * strips,))],
    )(enc_weight, dec_weight, enc_bias)
    far = move(whole, blks, toks, lambda b, t: ((FAR_0, FAR_1)[t % 2][b], t))
    (half,) = kernel_call(half_kernel, [pltpu.VMEM((STRIP, strips * width + TILE), BF16)], whole)
    one = move(half, blks, toks, lambda b, t: (NEAR[b], t))
    parts = 2
    *loaded, dec_bias = pl.pallas_call(
        load_kernel,
        out_shape=[pltpu.VMEM((tokens // parts, width), BF16)] * parts
        + [pltpu.VMEM((tokens // parts, width + latents), BF16)] * parts
        + [pltpu.VMEM(dec_bias.shape, F32)],
        in_specs=[pl.BlockSpec(memory_space=pl.ANY)] * 4 + [VMEM],
        out_specs=[VMEM] * (2 * parts + 1),
        scratch_shapes=[pltpu.VMEM(mask.shape, mask.dtype), pltpu.SemaphoreType.DMA((2 * parts + 2,))],
        cost_estimate=pl.CostEstimate(flops=0, bytes_accessed=4 * tokens * width, transcendentals=0),
    )(inputs, targets, mask, dec_bias, in_vmem(half))
    others = [swap(array) for array in loaded[::-1]][::-1]
    joined = kernel_call(
        join_kernel, [pltpu.VMEM((STRIP, 3 * strips * width + 2 * TILE), BF16)], far, one
    )
    other = swap(*joined)
    piece = (2 * rows, 2 * share)
    recon, *pieces, own = kernel_call(
        step_kernel,
        [pltpu.VMEM((tokens, width), BF16)]
        + [pltpu.VMEM(piece, BF16)] * len(CORE_1)
        + [pltpu.VMEM(piece, F32)],
        dec_bias, whole, one, far, other, *loaded, *others,
        scratch=[
            pltpu.VMEM((latents, width), BF16),
            pltpu.VMEM((latents, width), BF16),
            pltpu.VMEM((2 * tokens, width), BF16),
            pltpu.VMEM((latents, 2 * tokens), BF16),
            pltpu.VMEM((2 * tokens, width), BF16),
            pltpu.VMEM((latents, 2 * share), F32),
            pltpu.VMEM((latents, 2 * share), F32),
        ],
        flops=16 * tokens * latents * width,
    )
    arrived = []
    for zero, one_table, out in zip(CORE_0, CORE_1, pieces, strict=True):

        def where(b, t, tables=(zero, one_table)):
            to = tables[t % 2][b]
            return (to, t ^ 2 if t % 2 or to == b else t)

        arrived.append(move(out, blks, toks, where))
    send, keep = kernel_call(
        owner_kernel,
        [pltpu.VMEM((2 * rows, share), BF16), pltpu.VMEM((2 * rows, share), F32)],
        *arrived, own,
    )
    came = swap(send)
    grad_enc, grad_dec = kernel_call(
        lambda *refs: last_kernel(factor, *refs),
        [jax.ShapeDtypeStruct((rows, share), F32)] * 2,
        keep, came,
    )
    return recon, grad_enc, grad_dec


def large_body(inputs, targets, mask, enc_weight, enc_bias, dec_weight, dec_bias):
    gate = mask.astype(F32)
    enc_all = lax.all_gather(enc_weight, "blk", axis=0, tiled=True)
    dec_all = lax.all_gather(dec_weight, "blk", axis=0, tiled=True)
    bias_all = lax.all_gather(enc_bias, "blk", axis=0, tiled=True)
    pre = lax.dot_general(
        inputs, enc_all, (((1,), (1,)), ((), ())), preferred_element_type=F32
    )
    act = ((pre + bias_all.astype(F32)[None, :]) * gate).astype(BF16)
    recon_full = jnp.dot(act, dec_all, preferred_element_type=F32) + dec_bias[None, :]
    error = (recon_full - targets.astype(F32)).astype(BF16)
    back = lax.dot_general(
        error, dec_all, (((1,), (1,)), ((), ())), preferred_element_type=F32
    )
    dpre = (back * gate).astype(BF16)
    total = inputs.shape[0] * lax.axis_size("blk") * lax.axis_size("tok")
    factor = 1.0 / math.sqrt(total)
    grads = []
    for left, right in ((dpre, inputs), (act, error)):
        terms = lax.dot_general(
            left, right, (((0,), (0,)), ((), ())), preferred_element_type=F32
        )
        terms = lax.psum_scatter(terms, "blk", scatter_dimension=0, tiled=True)
        terms = lax.psum_scatter(terms, "tok", scatter_dimension=1, tiled=True)
        grads.append(terms * factor)
    return recon_full.astype(BF16), grads[0], grads[1]


def solution(mesh):
    small = mesh.shape["blk"] == 4 and mesh.shape["tok"] == 4
    tokens = P(("layers", "blk", "tok"), None)
    rows = P(("layers", "blk"), None)
    return jax.shard_map(
        small_body if small else large_body,
        mesh=mesh,
        in_specs=(tokens, tokens, tokens, rows, P(("layers", "blk")), rows, P("layers")),
        out_specs=(tokens, P(("layers", "blk"), "tok"), P(("layers", "blk"), "tok")),
        check_vma=False,
    )
```
